256 devices in a mesh: ctx: 32 (over y, x, core), exp: 8 (over z).
Axes of the slice: x: 4, y: 4, z: 8, core: 2. Of those that a mesh axis runs over, the one named last changes fastest.
Arguments:
- query: bfloat16 [2048, 4096], P('ctx', 'exp'), may hold values from -24 to 24
- key_states: bfloat16 [2048, 1024], P('ctx', 'exp'), may hold values from -24 to 24
- value_states: bfloat16 [2048, 1024], P('ctx', 'exp'), may hold values from -6 to 6
- residual: bfloat16 [2048, 4096], P('ctx'), may hold values from -6 to 6
- out_weight: bfloat16 [4096, 4096], P('exp'), may hold values from -0.09375 to 0.09375
- norm_gain: float32 [4096], replicated, may hold values from 0.1 to 1.9
- router_weight: bfloat16 [4096, 8], replicated, may hold values from -0.1875 to 0.1875
- expert_ids: int32 [2048, 2], P('ctx'), may hold values from 0 to 7, all different within a row; in each aligned block of 64 rows (0 to 63, 64 to 127, ...) at most 20 rows name the same one
- gate_weight: bfloat16 [8, 4096, 7168], P('exp', None, 'ctx'), may hold values from -0.09375 to 0.09375
- up_weight: bfloat16 [8, 4096, 7168], P('exp', None, 'ctx'), may hold values from -0.09375 to 0.09375
- down_weight: bfloat16 [8, 7168, 4096], P('exp', 'ctx'), may hold values from -0.0625 to 0.0625
Outputs:
- attended: bfloat16 [2048, 4096], P('ctx')
- expert_mix: bfloat16 [2048, 4096], P('ctx', 'exp')
The draws below stay inside these ranges and needn't reach their ends.
Inputs may be any that keep to these rules, and one draw needn't show every extreme that they name: `expert_ids`: in each aligned block of 64 rows (the tokens of one context shard) no expert is named by more than 20 rows, a bound that some block reaches; the two entries of a row differ.
All inputs are finite; a program needn't handle non-finite values.
Results may differ from the reference program's by a relative error of at most 0.034.
Values may be sent and summed in bfloat16 or wider, within the bound.
A program may use at most 64 MiB of HBM per device.

```python
import math
import jax
import jax.numpy as jnp
import numpy as np
from jax import lax

D = 4096
HEAD_DIM = 128
WINDOW = 4096
GROUP = 4
TOP = 2
FF_WIN = 7168
TOK_DEV = 64
SEQ = 2048
EXPERTS = 8
HEADS = 32
KV_HEADS = 8
CAP = 20
N_CTX = 32


def shared_base(key):
    return jnp.clip(jax.random.normal(key, (SEQ, KV_HEADS * HEAD_DIM), jnp.float32), -4.0, 4.0)


def draw_key_states(key, part):
    base = shared_base(key)
    return base.astype(jnp.bfloat16)


def draw_query(key, part):
    key = jax.random.fold_in(key, 5)
    own_rows = jnp.clip(jax.random.normal(key, (SEQ, HEADS * HEAD_DIM), jnp.float32), -4.0, 4.0)
    return own_rows.astype(jnp.bfloat16)


def steps_of(rng, dims, split, smallest, high):
    def one(dim, shards_of):
        draws = jax.random.uniform(jax.random.fold_in(jax.random.fold_in(rng, 6), dim), (shards_of,), jnp.float32, smallest / len(split), high / len(split))
        return jnp.repeat(jnp.exp(draws), dims[dim] // shards_of).reshape((-1,) + (1,) * (len(dims) - dim - 1))

    factor_of = one(*split[0])
    for cut in split[1:]:
        factor_of = factor_of * one(*cut)
    return factor_of


def assign_block(key, own, number, rows, number_of, top, bound, lean):
    ranking = jax.random.permutation(key, number_of)
    crowded, common = shares(number_of, rows * top, bound, lean, True), shares(number_of, rows * top, bound, lean, False)
    places = jnp.arange(number_of)

    def named(tallies, offset_by):
        used = int((tallies > 0).sum())
        fixed = max(1, used // 4)
        shifted = fixed + (places - fixed + offset_by * (used - fixed)) % max(1, number_of - fixed)
        return jnp.zeros((number_of,), jnp.int32).at[ranking[jnp.where(places < fixed, places, shifted)]].set(jnp.asarray(tallies, jnp.int32))

    tallies = jnp.where(number % 4 == 0, named(crowded, number // 4), named(common, number - number // 4 - 1))
    mixed = jax.random.permutation(jax.random.fold_in(own, 3), number_of)
    donor, sink = mixed[0:number_of // 2 * 2:2], mixed[1:number_of // 2 * 2:2]
    room = jnp.minimum(tallies[donor] - 1, bound - tallies[sink]) // 2
    room = jnp.where((donor == ranking[0]) | (sink == ranking[0]) | (tallies[sink] == 0), 0, jnp.maximum(room, 0))
    shifted = jax.random.randint(jax.random.fold_in(own, 4), (number_of // 2,), 0, 1 << 20) % (room + 1)
    tallies = tallies.at[donor].add(-shifted).at[sink].add(shifted)
    labels = jnp.searchsorted(jnp.cumsum(tallies), jnp.arange(rows * top), side="right").astype(jnp.int32)
    grid = labels.reshape(top, rows).T
    grid = grid[jax.random.permutation(jax.random.fold_in(own, 1), rows)]
    offset_by = jax.random.randint(jax.random.fold_in(own, 2), (rows, 1), 0, top)
    return jnp.take_along_axis(grid, (jnp.arange(top)[None, :] + offset_by) % top, axis=1)


def shares(count, total, bound, slope, full):
    weights = [(1 << 20) // math.isqrt(rank ** slope) + 1 for rank in range(1, count + 1)]
    largest = bound if full else min(bound, max(-(-total // count), total * weights[0] // sum(weights)))
    least = 1 if total - largest >= count - 1 else 0
    given, rest = [largest] + [least] * (count - 1), total - largest - least * (count - 1)
    while rest > 0:
        candidates = [i for i in range(1, count) if given[i] < largest] or [i for i in range(1, count) if given[i] < bound]
        pool, left = sum([weights[i] for i in candidates]), rest
        for i in candidates:
            more = min(bound - given[i], max(1, left * weights[i] // pool), rest)
            given[i] = given[i] + more
            rest = rest - more
    return np.array(given)


def centred(rng, dims, spread, limit, shards=(), kind=jnp.bfloat16):
    values = jax.random.normal(rng, dims, jnp.float32) * spread
    if len(shards) > 0:
        values = steps_of(rng, dims, shards, -0.22, 0.18) * values
    return jnp.clip(values, min=-limit, max=limit).astype(kind)


def setup_inputs(seed: int = 0) -> dict:
    key_of = jax.random.split(jax.random.key(seed), 12)
    query = draw_query(jax.random.fold_in(key_of[11], 71), 0)
    key_states = draw_key_states(jax.random.fold_in(key_of[11], 71), 0)
    value_states = centred(key_of[2], (SEQ, KV_HEADS * HEAD_DIM), 1.0, 6.0, ((0, 32), (1, 8)))
    residual = centred(key_of[3], (SEQ, D), 1.0, 6.0, ((0, 32),))
    out_weight = centred(key_of[4], (HEADS * HEAD_DIM, D), (HEADS * HEAD_DIM) ** -0.5, 0.09375, ((0, 8),))
    norm_gain = jnp.clip(1.0 + 0.18 * jax.random.normal(key_of[5], (D,), jnp.float32), 0.1, 1.9)
    router_weight = centred(key_of[6], (D, EXPERTS), (D // 4) ** -0.5, 0.1875)
    expert_ids_keys = jax.random.split(jax.random.fold_in(key_of[7], 1), SEQ // TOK_DEV)
    expert_ids_turns = jax.random.permutation(jax.random.fold_in(key_of[7], 3), SEQ // TOK_DEV)
    expert_ids = jax.vmap(lambda own, number: assign_block(jax.random.fold_in(key_of[7], 2), own, number, TOK_DEV, EXPERTS, TOP, CAP, 2))(expert_ids_keys, expert_ids_turns).reshape((SEQ, TOP))
    gate_weight = centred(key_of[8], (EXPERTS, D, FF_WIN), D ** -0.5, 0.09375, ((0, 8), (2, 32)))
    up_weight = centred(key_of[9], (EXPERTS, D, FF_WIN), D ** -0.5, 0.09375, ((0, 8), (2, 32)))
    down_weight = centred(key_of[10], (EXPERTS, FF_WIN, D), FF_WIN ** -0.5, 0.0625, ((0, 8), (1, 32)))
    return dict(query=query, key_states=key_states, value_states=value_states, residual=residual, out_weight=out_weight, norm_gain=norm_gain, router_weight=router_weight, expert_ids=expert_ids, gate_weight=gate_weight, up_weight=up_weight, down_weight=down_weight)


def reference(query, key_states, value_states, residual, out_weight, norm_gain, router_weight, expert_ids, gate_weight, up_weight, down_weight):
    score_scale = 1.0 / math.sqrt(HEAD_DIM)
    queries = query.astype(jnp.float32).reshape(N_CTX, TOK_DEV, KV_HEADS, GROUP, HEAD_DIM)
    key_rows = key_states.astype(jnp.float32).reshape(SEQ, KV_HEADS, HEAD_DIM)
    value_rows = value_states.astype(jnp.float32).reshape(SEQ, KV_HEADS, HEAD_DIM)
    positions = jnp.arange(SEQ, dtype=jnp.int32)

    def one_block(operands):
        block_queries, block_index = operands
        scores = jnp.einsum('tkgd,skd->tkgs', block_queries, key_rows, precision=lax.Precision.HIGHEST) * score_scale
        query_pos = block_index * TOK_DEV + jnp.arange(TOK_DEV, dtype=jnp.int32)
        allowed = (positions[None, :] <= query_pos[:, None]) & (positions[None, :] > query_pos[:, None] - WINDOW)
        allowed = allowed[:, None, None, :]
        scores = jnp.where(allowed, scores, -jnp.inf)
        largest = lax.optimization_barrier(jnp.max(scores, axis=-1, keepdims=True))
        weights = jnp.where(allowed, jnp.exp(scores - largest), 0.0)
        weight_sum = lax.optimization_barrier(jnp.sum(weights, axis=-1))
        weights_low = lax.optimization_barrier(weights.astype(jnp.bfloat16))
        mixed = jnp.einsum('tkgs,skd->tkgd', weights_low.astype(jnp.float32), value_rows, precision=lax.Precision.HIGHEST)
        return mixed / weight_sum[..., None]
    attention = lax.map(one_block, (queries, jnp.arange(N_CTX, dtype=jnp.int32)))
    attention = attention.reshape(SEQ, HEADS * HEAD_DIM).astype(jnp.bfloat16)
    attended = residual.astype(jnp.float32) + jnp.dot(attention, out_weight, preferred_element_type=jnp.float32)
    mean_square = lax.optimization_barrier(jnp.mean(attended * attended, axis=-1, keepdims=True))
    normed = (attended * lax.rsqrt(mean_square + 1e-05) * norm_gain).astype(jnp.bfloat16)
    logits = jnp.dot(normed, router_weight, preferred_element_type=jnp.float32)
    chosen = jnp.take_along_axis(logits, expert_ids, axis=1)
    first_gate = jax.nn.sigmoid(chosen[:, 0] - chosen[:, 1])
    gate_probs = jnp.stack([first_gate, 1.0 - first_gate], axis=1)
    routed = expert_ids.reshape(N_CTX, TOK_DEV * TOP)
    one_hot = (routed[..., None] == jnp.arange(EXPERTS, dtype=jnp.int32)).astype(jnp.int32)
    earlier = jnp.cumsum(one_hot, axis=1) - one_hot
    slot_index = lax.optimization_barrier(jnp.sum(earlier * one_hot, axis=-1)).astype(jnp.int32)
    shard_index = jnp.broadcast_to(jnp.arange(N_CTX, dtype=jnp.int32)[:, None], routed.shape)
    source = jnp.repeat(normed.reshape(N_CTX, TOK_DEV, D), TOP, axis=1)
    buffers = jnp.zeros((EXPERTS, N_CTX, CAP, D), normed.dtype).at[routed, shard_index, slot_index].set(source)

    def run_expert(operands):
        slot_rows, gate_part, up_part, down_part = operands
        slot_rows = slot_rows.reshape(N_CTX * CAP, D)
        gate = jnp.dot(slot_rows, gate_part, preferred_element_type=jnp.float32)
        upward = jnp.dot(slot_rows, up_part, preferred_element_type=jnp.float32)
        hidden = (jax.nn.silu(gate) * upward).astype(jnp.bfloat16)
        ranges = hidden.reshape(N_CTX * CAP, N_CTX, FF_WIN // N_CTX).transpose(1, 0, 2)
        downs = down_part.reshape(N_CTX, FF_WIN // N_CTX, D)

        def add_range(running, operands_pair):
            partial_value = jnp.dot(operands_pair[0], operands_pair[1], preferred_element_type=jnp.float32).astype(jnp.bfloat16)
            partial_value = lax.optimization_barrier(partial_value)
            return (running + partial_value.astype(jnp.float32), None)
        summed, unused = lax.scan(add_range, jnp.zeros((N_CTX * CAP, D), jnp.float32), (ranges, downs))
        return summed
    expert_out = lax.map(run_expert, (buffers, gate_weight, up_weight, down_weight)).reshape(EXPERTS, N_CTX, CAP, D)
    picked = expert_out[routed, shard_index, slot_index]
    weighted = picked * gate_probs.reshape(N_CTX, TOK_DEV * TOP)[..., None]
    expert_mix = lax.optimization_barrier(jnp.sum(weighted.reshape(N_CTX, TOK_DEV, TOP, D), axis=2)).reshape(SEQ, D).astype(jnp.bfloat16)
    return (attended.astype(jnp.bfloat16), expert_mix)
```

```python
import functools
import math

import jax
import jax.numpy as jnp
from jax import lax
from jax.experimental import pallas as pl
from jax.experimental.pallas import tpu as pltpu
from jax.sharding import PartitionSpec as P

WINDOW = 4096
SEQ = 2048
D = 4096
TOK = 64
CAP = 20
FF = 224
NZ = 8
COLS = D // NZ
HEAD = 128
GROUPS = 4
NB = 16
MAIN = 16
REM = CAP - MAIN
UNIT = COLS + 128
CUT = 384
BUNDLE = 4 * TOK
ROWS = NB * CAP
F32 = jnp.float32
BF16 = jnp.bfloat16
MESH = pl.DeviceIdType.MESH
HIGH = lax.Precision.HIGHEST
NT = (((1,), (1,)), ((), ()))

AG_LAGS = (1, 2, 3, 4)
RS_LAGS = (1, 2, 3, 4)


def iota(shape, dim):
    return lax.broadcasted_iota(jnp.int32, shape, dim)


def remote(src, dst, send, recv, device):
    return pltpu.make_async_remote_copy(
        src_ref=src, dst_ref=dst, send_sem=send, recv_sem=recv, device_id=device, device_id_type=MESH
    )


def wait(ref, sem):
    pltpu.make_async_copy(ref, ref, sem).wait()


def kernel(
    q_ref, k_ref, v_ref, res_ref, wo_ref, gain_ref, rt_ref, ids_ref, wg_ref, wu_ref, wd_ref,
    att_out, mix_out,
    qv, kv, qs, top, tot, acc, attn, wo, res, wg, wu, wd,
    sp, sm, rp, rm, att, ssum, lgt, place, perm, unperm,
    slots, scales, gate_acc, up_acc, hid, weight,
    part, r1p, r1m, r2p, r2m, r3p, r3m, r4p, r4m, yp, ym, tp, tm,
    ld, kvs, kvr, ws, wr, z1s, z1r, zas, zar, ags, agr, scs, scr, rss, rsr, z2s, z2r, outs,
):
    c = lax.axis_index("ctx")
    e = lax.axis_index("exp")
    core = lax.rem(c, 2)
    chip = lax.div(c, 2)
    x = lax.rem(chip, 4)
    y = lax.div(chip, 4)
    a = x + core * (y - x)
    b = y + core * (x - y)

    def ctx_of(aa, bb):
        return ((bb + core * (aa - bb)) * 4 + aa + core * (bb - aa)) * 2 + core

    ap, am, a2 = lax.rem(a + 1, 4), lax.rem(a + 3, 4), lax.rem(a + 2, 4)
    bp, bm, b2 = lax.rem(b + 1, 4), lax.rem(b + 3, 4), lax.rem(b + 2, 4)
    to_ap, to_am = (ctx_of(ap, b), e), (ctx_of(am, b), e)
    to_bp, to_bm = (ctx_of(a, bp), e), (ctx_of(a, bm), e)
    zp, zm = lax.rem(e + 1, NZ), lax.rem(e + NZ - 1, NZ)
    to_zp, to_zm = (c, zp), (c, zm)
    to_sib = (c + 1 - 2 * core, e)

    loads = [
        pltpu.make_async_copy(q_ref, qv, ld.at[0]),
        pltpu.make_async_copy(wo_ref, wo, ld.at[1]),
        pltpu.make_async_copy(
            res_ref.at[:, pl.ds(pl.multiple_of(e * COLS, COLS), COLS)], res, ld.at[2]
        ),
        pltpu.make_async_copy(wg_ref.at[0], wg.at[0:FF], ld.at[3]),
        pltpu.make_async_copy(wu_ref.at[0], wu.at[0:FF], ld.at[4]),
        pltpu.make_async_copy(wd_ref.at[0], wd.at[0:FF], ld.at[5]),
    ]

    def kv_rows(kk, bb, aa, units=1):
        return pl.ds(pl.multiple_of((kk * NB + bb * 4 + aa) * TOK, TOK), units * TOK)

    own = kv_rows(core, b, a)
    own_k = pltpu.make_async_copy(k_ref, kv.at[own, 0:HEAD], ld.at[6])
    own_v = pltpu.make_async_copy(v_ref, kv.at[own, HEAD : 2 * HEAD], ld.at[7])

    barrier = pltpu.get_barrier_semaphore()
    for other in (to_ap, to_am, to_bp, to_bm, to_zp, to_zm, to_sib):
        pl.semaphore_signal(barrier, inc=1, device_id=other, device_id_type=MESH)
    own_k.start()
    own_v.start()
    loads[0].start()
    pl.semaphore_wait(barrier, 7)

    k_own, v_own = kv.at[own, 0:HEAD], kv.at[own, HEAD : 2 * HEAD]
    kv_sent = []

    def kv_send(src, dst, i, device, recv=None):
        copy = remote(src, dst, kvs.at[len(kv_sent)], kvr.at[i], device)
        copy.start()
        kv_sent.append((dst, len(kv_sent)))

    kv_send(k_ref, k_own, 0, to_ap)
    kv_send(v_ref, v_own, 3, to_am)
    kv_send(v_ref, v_own, 1, to_ap)
    kv_send(k_ref, k_own, 2, to_am)
    for copy in loads[1:]:
        copy.start()
    w_sent = []
    for i, (src, dst) in enumerate(((wg_ref, wg), (wu_ref, wu), (wd_ref, wd))):
        copy = remote(src.at[0], dst.at[FF : 2 * FF], ws.at[i], wr.at[i], to_sib)
        copy.start()
        w_sent.append((dst.at[FF : 2 * FF], i))

    ids = ids_ref[...]
    first_id, second_id = ids[0:1, :], ids[1:2, :]
    mine = jnp.where((first_id == e) | (second_id == e), 1.0, 0.0)
    before = jnp.where(iota((TOK, TOK), 0) < iota((TOK, TOK), 1), 1.0, 0.0).astype(BF16)
    slot = jnp.dot(
        jnp.broadcast_to(mine, (8, TOK)).astype(BF16), before, preferred_element_type=F32
    )[0:1, :]
    slot = jnp.where(mine > 0.0, slot, -1.0)
    row = iota((2 * MAIN, TOK), 0)
    wanted = jnp.where(row < MAIN, row, MAIN + lax.rem(row, REM)).astype(F32)
    place[...] = jnp.where(jnp.broadcast_to(slot, (2 * MAIN, TOK)) == wanted, 1.0, 0.0).astype(BF16)
    by_token = jnp.where(
        jnp.broadcast_to(slot, (HEAD, TOK)) == iota((HEAD, TOK), 0).astype(F32), 1.0, 0.0
    ).astype(BF16)
    eye = jnp.where(iota((TOK, TOK), 0) == iota((TOK, TOK), 1), 1.0, 0.0)
    slot_of_token = lax.dot_general(eye.astype(BF16), by_token, NT, preferred_element_type=F32)

    r256, l256 = iota((256, 256), 0), iota((256, 256), 1)
    i64 = lax.rem(r256, 64)
    to_unit = lax.div(i64, REM) * 16 + lax.div(r256, 64) * REM + lax.rem(i64, REM)
    perm[...] = jnp.where(l256 == to_unit, 1.0, 0.0).astype(BF16)
    to_flat = lax.rem(lax.div(r256, REM), 4) * 64 + lax.div(r256, 16) * REM + lax.rem(r256, REM)
    unperm[...] = jnp.where(l256 == to_flat, 1.0, 0.0).astype(BF16)

    gate_acc[...] = jnp.zeros_like(gate_acc)
    up_acc[...] = jnp.zeros_like(up_acc)
    ssum[...] = jnp.zeros_like(ssum)
    lgt[...] = jnp.zeros_like(lgt)
    half = COLS // 2
    tp[0, :, half:] = jnp.zeros((TOK, half), BF16)
    tm[0, :, :half] = jnp.zeros((TOK, half), BF16)
    top[...] = jnp.full(top.shape, -1e30, F32)
    tot[...] = jnp.zeros_like(tot)
    acc[...] = jnp.zeros_like(acc)

    loads[0].wait()
    for g in range(GROUPS):
        qs[g * TOK : (g + 1) * TOK, :] = qv[:, g * HEAD : (g + 1) * HEAD]

    rows_m, rows_p, rows_2 = kv_rows(core, b, am), kv_rows(core, b, ap), kv_rows(core, b, a2)
    klane, vlane = slice(0, HEAD), slice(HEAD, 2 * HEAD)
    wait(kv.at[rows_m, klane], kvr.at[0])
    kv_send(kv.at[rows_m, klane], kv.at[rows_m, klane], 4, to_ap)
    wait(kv.at[rows_p, vlane], kvr.at[3])
    kv_send(kv.at[rows_p, vlane], kv.at[rows_p, vlane], 5, to_am)
    wait(kv.at[rows_m, vlane], kvr.at[1])
    wait(kv.at[rows_p, klane], kvr.at[2])
    own_k.wait()
    own_v.wait()
    wait(kv.at[rows_2, klane], kvr.at[4])
    wait(kv.at[rows_2, vlane], kvr.at[5])
    whole = kv_rows(core, b, 0, 4)
    kv_send(kv.at[whole, :], kv.at[whole, :], 6, to_bp)
    kv_send(kv.at[whole, :], kv.at[whole, :], 7, to_bm)
    kv_send(kv.at[whole, :], kv.at[whole, :], 10, to_sib)

    query_pos = c * TOK + lax.rem(iota((GROUPS * TOK, 1), 0), TOK)
    lane = iota((1, BUNDLE), 1)
    score_scale = 1.0 / math.sqrt(HEAD)

    def attend(kk, bb):
        rows = kv_rows(kk, bb, 0, 4)
        key_pos = (
            TOK * kk
            + lax.rem(lane, TOK)
            + 2 * TOK * ((1 + 3 * kk) * lax.div(lane, TOK) + (4 - 3 * kk) * bb)
        )
        scores = (
            lax.dot_general(qs[...], kv[rows, klane], NT, preferred_element_type=F32) * score_scale
        )
        allowed = key_pos <= query_pos
        if SEQ > WINDOW:
            allowed = allowed & (key_pos > query_pos - WINDOW)
        scores = jnp.where(allowed, scores, -1e30)
        old = top[:, 0:1]
        new = jnp.maximum(old, jnp.max(scores, axis=1, keepdims=True))
        fade = jnp.exp(old - new)
        weights = jnp.exp(scores - new)
        top[...] = jnp.broadcast_to(new, top.shape)
        tot[...] = tot[...] * fade + jnp.sum(weights, axis=1, keepdims=True)
        acc[...] = acc[...] * fade + jnp.dot(
            weights.astype(BF16), kv[rows, vlane], preferred_element_type=F32
        )

    def other_wait(aa, i):
        wait(kv.at[kv_rows(1 - core, aa, 0, 4), :], kvr.at[i])

    def halves(bb):
        first = pl.multiple_of((core * NB + bb * 4) * TOK, TOK)
        return pl.ds(first, 2 * TOK), pl.ds(pl.multiple_of(first + 2 * TOK, TOK), 2 * TOK)

    attend(core, b)
    other_wait(a, 10)
    attend(1 - core, a)
    whole_m, whole_p, whole_2 = (kv_rows(core, bb, 0, 4) for bb in (bm, bp, b2))
    wait(kv.at[whole_m, :], kvr.at[6])
    kv_send(kv.at[halves(bm)[0], :], kv.at[halves(bm)[0], :], 8, to_bp)
    kv_send(kv.at[whole_m, :], kv.at[whole_m, :], 11, to_sib)
    wait(kv.at[whole_p, :], kvr.at[7])
    kv_send(kv.at[halves(bp)[1], :], kv.at[halves(bp)[1], :], 9, to_bm)
    kv_send(kv.at[whole_p, :], kv.at[whole_p, :], 12, to_sib)
    attend(core, bm)
    attend(core, bp)
    wait(kv.at[halves(b2)[0], :], kvr.at[8])
    wait(kv.at[halves(b2)[1], :], kvr.at[9])
    kv_send(kv.at[whole_2, :], kv.at[whole_2, :], 13, to_sib)
    other_wait(am, 11)
    attend(1 - core, am)
    other_wait(ap, 12)
    attend(1 - core, ap)
    attend(core, b2)
    other_wait(a2, 13)
    attend(1 - core, a2)

    for g in range(GROUPS):
        rows = slice(g * TOK, (g + 1) * TOK)
        attn[:, g * HEAD : (g + 1) * HEAD] = (acc[rows, :] / tot[rows, 0:1]).astype(BF16)

    def chunk(s):
        return lax.rem(e + s + NZ, NZ)

    def cols(j):
        return pl.ds(pl.multiple_of(j * COLS, COLS), COLS)

    def project(s):
        return jnp.dot(attn[...], wo[:, cols(chunk(s))], preferred_element_type=F32)

    lo, hi = slice(0, half), slice(half, COLS)
    loads[1].wait()
    far = project(4).astype(BF16)
    sp[0] = far
    remote(sp.at[0, :, lo], rp.at[0, :, lo], z1s.at[0], z1r.at[0], to_zp).start()
    remote(sp.at[0, :, hi], rm.at[0, :, hi], z1s.at[4], z1r.at[4], to_zm).start()
    for i in range(1, 4):
        up, down = project(4 - i), project(i - 4)
        if i == 1:
            wait(rp.at[0, :, lo], z1r.at[0])
            sp[1, :, lo] = (up[:, lo] + rp[0, :, lo].astype(F32)).astype(BF16)
            sp[1, :, hi] = up[:, hi].astype(BF16)
        else:
            wait(rp.at[i - 1], z1r.at[i - 1])
            sp[i] = (up + rp[i - 1].astype(F32)).astype(BF16)
        remote(sp.at[i], rp.at[i], z1s.at[i], z1r.at[i], to_zp).start()
        if i == 1:
            wait(rm.at[0, :, hi], z1r.at[4])
            sm[1, :, hi] = (down[:, hi] + rm[0, :, hi].astype(F32)).astype(BF16)
            sm[1, :, lo] = down[:, lo].astype(BF16)
        else:
            wait(rm.at[i - 1], z1r.at[4 + i - 1])
            sm[i] = (down + rm[i - 1].astype(F32)).astype(BF16)
        remote(sm.at[i], rm.at[i], z1s.at[4 + i], z1r.at[4 + i], to_zm).start()
    loads[2].wait()
    total = project(0) + res[...].astype(F32)
    wait(rp.at[3], z1r.at[3])
    wait(rm.at[3], z1r.at[7])
    att[e] = (total + rp[3].astype(F32) + rm[3].astype(F32)).astype(BF16)
    remote(att.at[e], att.at[e], zas.at[0], zar.at[2], to_zp).start()
    remote(att.at[e], att.at[e], zas.at[7], zar.at[1], to_zm).start()

    def ag_chunk(n):
        odd = lax.rem(n, 2)
        return chunk((2 * odd - 1) * lax.div(n + 1, 2))

    def unit(aa, bb):
        return pl.ds(pl.multiple_of((bb * 4 + aa) * MAIN, MAIN), MAIN)

    def bundle(bb):
        return pl.ds(pl.multiple_of(bb * 64, 64), 64)

    def first_half(bb):
        return pl.ds(pl.multiple_of(bb * 64, 32), 32)

    def second_half(bb):
        return pl.ds(pl.multiple_of(bb * 64 + 32, 32), 32)

    def scale_unit(aa, bb):
        return pl.ds(pl.multiple_of((bb * 4 + aa) * 8, 8), 8)

    def scale_bundle(bb):
        return pl.ds(pl.multiple_of(bb * 32, 8), 32)

    def out_copy(j):
        return pltpu.make_async_copy(att.at[j], att_out.at[:, cols(j)], outs.at[j])

    def left(rows, cut):
        return rows, slice(0, cut)

    def ag_start(n):
        j = ag_chunk(n)
        odd = lax.rem(n, 2)

        @pl.when((n > 0) & (n < 7))
        def _():
            wait(att.at[j], zar.at[n])

        @pl.when((n > 0) & (n < 5))
        def _():
            remote(
                att.at[j], att.at[j], zas.at[n], zar.at[n + 2], (c, lax.rem(e + 1 - 2 * odd + NZ, NZ))
            ).start()

        @pl.when(n == 5)
        def _():
            remote(att.at[j, :, hi], att.at[j, :, hi], zas.at[5], zar.at[8], to_zm).start()

        @pl.when(n == 6)
        def _():
            remote(att.at[j, :, lo], att.at[j, :, lo], zas.at[6], zar.at[7], to_zp).start()

        @pl.when(n == 7)
        def _():
            wait(att.at[j, :, lo], zar.at[7])
            wait(att.at[j, :, hi], zar.at[8])

        out_copy(j).start()
        value = att[j].astype(F32)
        scaled = (value * gain_ref[:, cols(j)]).astype(BF16)
        packed = jnp.dot(place[...], scaled, preferred_element_type=F32)
        mine_rows = unit(a, b)
        slots[j, mine_rows, 0:COLS] = packed[0:MAIN].astype(BF16)
        tile = lax.div(iota((MAIN, 128), 0), REM)
        rest = jnp.zeros((MAIN, 128), F32)
        for t in range(4):
            rest = rest + jnp.where(tile == t, packed[MAIN:, t * 128 : (t + 1) * 128], 0.0)
        slots[j, mine_rows, COLS:UNIT] = rest.astype(BF16)
        here = slots.at[j, mine_rows, :]
        remote(here, here, ags.at[0, n], agr.at[0, n], to_ap).start()
        remote(here, here, ags.at[1, n], agr.at[1, n], to_am).start()
        ssum[...] += jnp.sum(value * value, axis=1, keepdims=True)
        lgt[...] += lax.dot_general(rt_ref[:, cols(j)], scaled, NT, preferred_element_type=F32)

        @pl.when(n == 7)
        def _():
            inverse = lax.rsqrt(ssum[:, 0:1] * (1.0 / D) + 1e-05)
            by_slot = jnp.sum(slot_of_token * inverse, axis=0, keepdims=True)
            scales[scale_unit(a, b), :] = jnp.broadcast_to(by_slot, (8, HEAD))
            here = scales.at[scale_unit(a, b), :]
            remote(here, here, scs.at[0], scr.at[0], to_ap).start()
            remote(here, here, scs.at[1], scr.at[1], to_am).start()
            inverse_row = jnp.sum(eye * inverse, axis=0, keepdims=True)
            logits = lgt[...] * inverse_row
            number = iota((NZ, TOK), 0)
            one = jnp.sum(jnp.where(number == first_id, logits, 0.0), axis=0, keepdims=True)
            two = jnp.sum(jnp.where(number == second_id, logits, 0.0), axis=0, keepdims=True)
            gate = 1.0 / (1.0 + jnp.exp(two - one))
            gate = jnp.where(first_id == e, gate, 1.0 - gate)
            spread = jnp.where(
                jnp.broadcast_to(slot, (2 * MAIN, TOK)) == wanted,
                jnp.broadcast_to(gate, (2 * MAIN, TOK)),
                0.0,
            )
            weight[...] = lax.dot_general(
                eye, spread, NT, precision=HIGH, preferred_element_type=F32
            )

    def ag_first(n):
        j = ag_chunk(n)
        at_m, at_p = unit(am, b), unit(ap, b)
        wait(slots.at[j, at_m, :], agr.at[0, n])
        piece = slots.at[j, at_m, 0:CUT]
        remote(piece, piece, ags.at[2, n], agr.at[2, n], to_ap).start()
        wait(slots.at[j, at_p, :], agr.at[1, n])
        piece = slots.at[j, at_p, CUT:UNIT]
        remote(piece, piece, ags.at[3, n], agr.at[3, n], to_am).start()

        @pl.when(n == 7)
        def _():
            piece = scales.at[scale_unit(am, b), :]
            wait(piece, scr.at[0])
            remote(piece, piece, scs.at[2], scr.at[2], to_ap).start()
            wait(scales.at[scale_unit(ap, b), :], scr.at[1])

    def ag_second(n):
        j = ag_chunk(n)
        at_2 = unit(a2, b)
        wait(slots.at[j, at_2, 0:CUT], agr.at[2, n])
        wait(slots.at[j, at_2, CUT:UNIT], agr.at[3, n])
        piece = slots.at[j, bundle(b), :]
        remote(piece, piece, ags.at[4, n], agr.at[4, n], to_bp).start()
        remote(piece, piece, ags.at[5, n], agr.at[5, n], to_bm).start()

        @pl.when(n == 7)
        def _():
            wait(scales.at[scale_unit(a2, b), :], scr.at[2])
            piece = scales.at[scale_bundle(b), :]
            remote(piece, piece, scs.at[3], scr.at[3], to_bp).start()
            remote(piece, piece, scs.at[4], scr.at[4], to_bm).start()

    def ag_third(n):
        j = ag_chunk(n)
        wait(slots.at[j, bundle(bm), :], agr.at[4, n])
        piece = slots.at[j, first_half(bm), :]
        remote(piece, piece, ags.at[6, n], agr.at[6, n], to_bp).start()
        wait(slots.at[j, bundle(bp), :], agr.at[5, n])
        piece = slots.at[j, second_half(bp), :]
        remote(piece, piece, ags.at[7, n], agr.at[7, n], to_bm).start()

        @pl.when(n == 7)
        def _():
            piece = scales.at[scale_bundle(bm), :]
            wait(piece, scr.at[3])
            remote(piece, piece, scs.at[5], scr.at[5], to_bp).start()
            wait(scales.at[scale_bundle(bp), :], scr.at[4])

    def ag_use(n):
        j = ag_chunk(n)
        wait(slots.at[j, first_half(b2), :], agr.at[6, n])
        wait(slots.at[j, second_half(b2), :], agr.at[7, n])
        flat = jnp.dot(
            perm[...], slots[j, 0:256, COLS:UNIT], preferred_element_type=F32
        ).astype(BF16)
        for t in range(4):
            slots[j, 256:ROWS, t * 128 : (t + 1) * 128] = flat[t * 64 : (t + 1) * 64]
        rows = slots[j, :, 0:COLS]
        gate_acc[...] += lax.dot_general(rows, wg[:, cols(j)], NT, preferred_element_type=F32)
        up_acc[...] += lax.dot_general(rows, wu[:, cols(j)], NT, preferred_element_type=F32)

    def run(stages, count):
        last = max(lag for _, lag in stages)

        def tick(t, carry):
            for function, lag in stages:

                @pl.when((t >= lag) & (t < lag + count))
                def _(function=function, lag=lag):
                    function(t - lag)

            return carry

        lax.fori_loop(0, count + last, tick, 0)

    loads[3].wait()
    loads[4].wait()
    wait(wg.at[FF : 2 * FF], wr.at[0])
    wait(wu.at[FF : 2 * FF], wr.at[1])
    run(
        (
            (ag_third, AG_LAGS[2]),
            (ag_second, AG_LAGS[1]),
            (ag_first, AG_LAGS[0]),
            (ag_start, 0),
            (ag_use, AG_LAGS[3]),
        ),
        NZ,
    )
    wait(scales.at[scale_bundle(b2), :], scr.at[5])

    row = iota((ROWS, HEAD), 0)
    col = iota((ROWS, HEAD), 1)
    over = row - 256
    block_of = jnp.where(row < 256, lax.div(row, MAIN), lax.div(over, REM))
    slot_of = jnp.where(row < 256, lax.rem(row, MAIN), MAIN + lax.rem(over + 256, REM))
    pick = jnp.where(col == block_of * 8, 1.0, 0.0)
    spread = jnp.dot(pick, scales[...], precision=HIGH, preferred_element_type=F32)
    factor = jnp.sum(jnp.where(col == slot_of, spread, 0.0), axis=1, keepdims=True)
    gated = gate_acc[...] * factor
    hid[...] = (gated / (1.0 + jnp.exp(-gated)) * (up_acc[...] * factor)).astype(BF16)
    loads[5].wait()
    wait(wd.at[FF : 2 * FF], wr.at[2])

    def rs_chunk(n):
        odd = lax.rem(n, 2)
        return chunk(odd * (4 - lax.div(n + 1, 2)) - (1 - odd) * (4 - lax.div(n, 2)))

    def rs_start(n):
        j = rs_chunk(n)
        out = jnp.dot(hid[...], wd[:, cols(j)], preferred_element_type=F32).astype(BF16)
        part[n, :, 0:COLS] = out[0:256]
        rest = jnp.concatenate([out[256:, t * 128 : (t + 1) * 128] for t in range(4)], axis=0)
        part[n, :, COLS:UNIT] = jnp.dot(unperm[...], rest, preferred_element_type=F32).astype(BF16)
        remote(
            part.at[n, first_half(b2), :], r1p.at[n], rss.at[0, n], rsr.at[0, n], to_bp
        ).start()
        remote(
            part.at[n, second_half(b2), :], r1m.at[n], rss.at[1, n], rsr.at[1, n], to_bm
        ).start()

    def add(n, rows, lanes, more):
        value = part[n, rows, lanes].astype(F32)
        for term in more:
            value = value + term.astype(F32)
        return value

    every = slice(0, UNIT)

    def rs_first(n):
        wait(r1p.at[n], rsr.at[0, n])
        rows = first_half(bp)
        part[n, rows, every] = add(n, rows, every, [r1p[n]]).astype(BF16)
        remote(part.at[n, bundle(bp), :], r2p.at[n], rss.at[2, n], rsr.at[2, n], to_bp).start()
        wait(r1m.at[n], rsr.at[1, n])
        rows = second_half(bm)
        part[n, rows, every] = add(n, rows, every, [r1m[n]]).astype(BF16)
        remote(part.at[n, bundle(bm), :], r2m.at[n], rss.at[3, n], rsr.at[3, n], to_bm).start()

    def rs_second(n):
        wait(r2p.at[n], rsr.at[2, n])
        wait(r2m.at[n], rsr.at[3, n])
        rows = bundle(b)
        part[n, rows, every] = add(n, rows, every, [r2p[n], r2m[n]]).astype(BF16)
        at_2 = unit(a2, b)
        remote(
            part.at[n, at_2, 0:CUT], r3p.at[n], rss.at[4, n], rsr.at[4, n], to_ap
        ).start()
        remote(
            part.at[n, at_2, CUT:UNIT], r3m.at[n], rss.at[5, n], rsr.at[5, n], to_am
        ).start()

    def rs_third(n):
        at_p, at_m = unit(ap, b), unit(am, b)
        wait(r3p.at[n], rsr.at[4, n])
        part[n, at_p, 0:CUT] = add(n, at_p, slice(0, CUT), [r3p[n]]).astype(BF16)
        remote(part.at[n, at_p, :], r4p.at[n], rss.at[6, n], rsr.at[6, n], to_ap).start()
        wait(r3m.at[n], rsr.at[5, n])
        part[n, at_m, CUT:UNIT] = add(n, at_m, slice(CUT, UNIT), [r3m[n]]).astype(BF16)
        remote(part.at[n, at_m, :], r4m.at[n], rss.at[7, n], rsr.at[7, n], to_am).start()

    def rs_last(n):
        wait(r4p.at[n], rsr.at[6, n])
        wait(r4m.at[n], rsr.at[7, n])
        mine_sum = add(n, unit(a, b), every, [r4p[n], r4m[n]])
        tile = lax.div(iota((MAIN, 128), 0), REM)
        rest = jnp.concatenate(
            [jnp.where(tile == t, mine_sum[:, COLS:UNIT], 0.0) for t in range(4)], axis=1
        )
        terms = jnp.concatenate([mine_sum[:, 0:COLS], rest], axis=0)
        mixed = jnp.dot(weight[...], terms, precision=HIGH, preferred_element_type=F32)
        odd = lax.rem(n, 2)
        i = lax.div(n + 1, 2)

        @pl.when(n == 0)
        def _():
            yp[0] = mixed.astype(BF16)
            remote(yp.at[0, :, lo], tp.at[0, :, lo], z2s.at[0], z2r.at[0], to_zp).start()
            remote(yp.at[0, :, hi], tm.at[0, :, hi], z2s.at[4], z2r.at[4], to_zm).start()

        @pl.when(n == 1)
        def _():
            wait(tp.at[0, :, lo], z2r.at[0])

        @pl.when(n == 2)
        def _():
            wait(tm.at[0, :, hi], z2r.at[4])

        @pl.when((n > 2) & (odd == 1))
        def _():
            wait(tp.at[i - 1], z2r.at[i - 1])

        @pl.when((n > 2) & (odd == 0))
        def _():
            wait(tm.at[i - 1], z2r.at[4 + i - 1])

        @pl.when((n < 7) & (odd == 1))
        def _():
            yp[i] = (mixed + tp[i - 1].astype(F32)).astype(BF16)
            remote(yp.at[i], tp.at[i], z2s.at[i], z2r.at[i], to_zp).start()

        @pl.when((n > 0) & (odd == 0))
        def _():
            ym[i] = (mixed + tm[i - 1].astype(F32)).astype(BF16)
            remote(ym.at[i], tm.at[i], z2s.at[4 + i], z2r.at[4 + i], to_zm).start()

        @pl.when(n == 7)
        def _():
            wait(tm.at[3], z2r.at[7])
            mix_out[...] = (mixed + tp[3].astype(F32) + tm[3].astype(F32)).astype(BF16)

    run(
        (
            (rs_last, RS_LAGS[3]),
            (rs_third, RS_LAGS[2]),
            (rs_second, RS_LAGS[1]),
            (rs_first, RS_LAGS[0]),
            (rs_start, 0),
        ),
        NZ,
    )

    for ref, i in kv_sent:
        wait(ref, kvs.at[i])
    for ref, i in w_sent:
        wait(ref, ws.at[i])
    for i in range(8):
        part_of = (slice(None), lo) if i == 0 else (slice(None), hi) if i == 4 else (slice(None),) * 2
        wait(sp.at[(0,) + part_of], z1s.at[i])
        wait(yp.at[(0,) + part_of], z2s.at[i])

    def drain(n, carry):
        for i, piece in enumerate(
            (
                slots.at[0, 0:MAIN, :], slots.at[0, 0:MAIN, :], slots.at[0, 0:MAIN, 0:CUT],
                slots.at[0, 0:MAIN, CUT:UNIT], slots.at[0, 0:64, :], slots.at[0, 0:64, :],
                slots.at[0, 0:32, :], slots.at[0, 0:32, :],
            )
        ):
            wait(piece, ags.at[i, n])
        for i, piece in enumerate((r1p, r1m, r2p, r2m, r3p, r3m, r4p, r4m)):
            wait(piece.at[0], rss.at[i, n])
        out_copy(n).wait()
        return carry

    lax.fori_loop(0, NZ, drain, 0)
    for i in range(8):
        piece = att.at[0, :, hi] if i == 5 else att.at[0, :, lo] if i == 6 else att.at[0]
        wait(piece, zas.at[i])
    for i in range(6):
        wait(scales.at[0:8, :] if i < 3 else scales.at[0:32, :], scs.at[i])


def local(
    query, key_states, value_states, residual, out_weight, norm_gain, router_weight, expert_ids,
    gate_weight, up_weight, down_weight,
):
    anywhere = pl.BlockSpec(memory_space=pl.ANY)
    near = pl.BlockSpec(memory_space=pltpu.VMEM)
    vmem = pltpu.VMEM
    dma = pltpu.SemaphoreType.DMA
    scratch = [
        vmem((TOK, GROUPS * HEAD), BF16),
        vmem((SEQ, 2 * HEAD), BF16),
        vmem((GROUPS * TOK, HEAD), BF16),
        vmem((GROUPS * TOK, HEAD), F32),
        vmem((GROUPS * TOK, HEAD), F32),
        vmem((GROUPS * TOK, HEAD), F32),
        vmem((TOK, GROUPS * HEAD), BF16),
        vmem((GROUPS * HEAD, D), BF16),
        vmem((TOK, COLS), BF16),
        vmem((2 * FF, D), BF16),
        vmem((2 * FF, D), BF16),
        vmem((2 * FF, D), BF16),
        vmem((4, TOK, COLS), BF16),
        vmem((4, TOK, COLS), BF16),
        vmem((4, TOK, COLS), BF16),
        vmem((4, TOK, COLS), BF16),
        vmem((NZ, TOK, COLS), BF16),
        vmem((TOK, HEAD), F32),
        vmem((NZ, TOK), F32),
        vmem((2 * MAIN, TOK), BF16),
        vmem((256, 256), BF16),
        vmem((256, 256), BF16),
        vmem((NZ, ROWS, UNIT), BF16),
        vmem((NB * 8, HEAD), F32),
        vmem((ROWS, 2 * FF), F32),
        vmem((ROWS, 2 * FF), F32),
        vmem((ROWS, 2 * FF), BF16),
        vmem((TOK, 2 * MAIN), F32),
        vmem((NZ, 256, UNIT), BF16),
        vmem((NZ, 32, UNIT), BF16),
        vmem((NZ, 32, UNIT), BF16),
        vmem((NZ, 64, UNIT), BF16),
        vmem((NZ, 64, UNIT), BF16),
        vmem((NZ, MAIN, CUT), BF16),
        vmem((NZ, MAIN, UNIT - CUT), BF16),
        vmem((NZ, MAIN, UNIT), BF16),
        vmem((NZ, MAIN, UNIT), BF16),
        vmem((4, TOK, COLS), BF16),
        vmem((4, TOK, COLS), BF16),
        vmem((4, TOK, COLS), BF16),
        vmem((4, TOK, COLS), BF16),
        dma((8,)),
        dma((14,)),
        dma((14,)),
        dma((3,)),
        dma((3,)),
        dma((8,)),
        dma((8,)),
        dma((8,)),
        dma((9,)),
        dma((8, NZ)),
        dma((8, NZ)),
        dma((6,)),
        dma((6,)),
        dma((8, NZ)),
        dma((8, NZ)),
        dma((8,)),
        dma((8,)),
        dma((NZ,)),
    ]
    return pl.pallas_call(
        kernel,
        out_shape=(
            jax.ShapeDtypeStruct((TOK, D), BF16),
            jax.ShapeDtypeStruct((TOK, COLS), BF16),
        ),
        in_specs=[anywhere] * 5 + [near] * 3 + [anywhere] * 3,
        out_specs=(anywhere, near),
        scratch_shapes=scratch,
        compiler_params=pltpu.CompilerParams(
            collective_id=0, has_side_effects=True, vmem_limit_bytes=56 * 1024 * 1024
        ),
        name="layer",
    )(
        query,
        key_states,
        value_states,
        residual,
        out_weight,
        norm_gain.reshape(1, D),
        router_weight.T,
        expert_ids.T,
        jnp.swapaxes(gate_weight, 1, 2),
        jnp.swapaxes(up_weight, 1, 2),
        down_weight,
    )


def solution(mesh):
    placed = (
        P("ctx", "exp"),
        P("ctx", "exp"),
        P("ctx", "exp"),
        P("ctx", None),
        P("exp", None),
        P(),
        P(),
        P("ctx", None),
        P("exp", None, "ctx"),
        P("exp", None, "ctx"),
        P("exp", "ctx", None),
    )
    return jax.shard_map(
        local,
        mesh=mesh,
        in_specs=placed,
        out_specs=(P("ctx", None), P("ctx", "exp")),
        check_vma=False,
    )
```

```python
import functools
import math

import jax
import jax.numpy as jnp
from jax import lax
from jax.experimental import pallas as pl
from jax.experimental.pallas import tpu as pltpu
from jax.sharding import PartitionSpec as P

WINDOW = 4096
SEQ = 2048
D = 4096
TOK = 64
CAP = 20
FF = 224
NZ = 8
COLS = D // NZ
HEAD = 128
GROUPS = 4
NB = 16
MAIN = 16
REM = CAP - MAIN
UNIT = COLS + 128
BUNDLE = 4 * TOK
ROWS = NB * CAP
F32 = jnp.float32
BF16 = jnp.bfloat16
MESH = pl.DeviceIdType.MESH
HIGH = lax.Precision.HIGHEST
NT = (((1,), (1,)), ((), ()))

AG_LAGS = (3, 6, 9)
RS_LAGS = (3, 6, 9)
AG_RELAYED = 6
RS_RELAYED = 6


def iota(shape, dim):
    return lax.broadcasted_iota(jnp.int32, shape, dim)


def remote(src, dst, send, recv, device):
    return pltpu.make_async_remote_copy(
        src_ref=src, dst_ref=dst, send_sem=send, recv_sem=recv, device_id=device, device_id_type=MESH
    )


def wait(ref, sem):
    pltpu.make_async_copy(ref, ref, sem).wait()


def kernel(
    q_ref, k_ref, v_ref, res_ref, wo_ref, gain_ref, rt_ref, ids_ref, wg_ref, wu_ref, wd_ref,
    att_out, mix_out,
    qv, kv, qs, top, tot, acc, attn, wo, res, wg, wu, wd,
    zs, zr, att, stats, place, perm, unperm, zunits,
    slots, scales, gate_acc, up_acc, hid, wgt_hi, wgt_lo,
    part, r1p, r1m, r2p, r2m, r2x, r4p, r4m, r4x, zout, fin, terms,
    ld, kvs, kvr, ws, wr, z1s, z1r, zas, zar, sts, str_, ats, atr, ags, agr, scs, scr, rss, rsr,
    z2s, z2r, outs,
):
    c = lax.axis_index("ctx")
    e = lax.axis_index("exp")
    core = lax.rem(c, 2)
    chip = lax.div(c, 2)
    x = lax.rem(chip, 4)
    y = lax.div(chip, 4)
    a = x + core * (y - x)
    b = y + core * (x - y)

    def ctx_of(aa, bb):
        return ((bb + core * (aa - bb)) * 4 + aa + core * (bb - aa)) * 2 + core

    ap, am, a2 = lax.rem(a + 1, 4), lax.rem(a + 3, 4), lax.rem(a + 2, 4)
    bp, bm, b2 = lax.rem(b + 1, 4), lax.rem(b + 3, 4), lax.rem(b + 2, 4)
    to_ap, to_am, to_a2 = (ctx_of(ap, b), e), (ctx_of(am, b), e), (ctx_of(a2, b), e)
    to_bp, to_bm, to_b2 = (ctx_of(a, bp), e), (ctx_of(a, bm), e), (ctx_of(a, b2), e)

    def chunk(s):
        return lax.rem(e + s + NZ, NZ)

    def to_z(s):
        return (c, chunk(s))

    to_sib = (c + 1 - 2 * core, e)

    loads = [
        pltpu.make_async_copy(q_ref, qv, ld.at[0]),
        pltpu.make_async_copy(wo_ref, wo, ld.at[1]),
        pltpu.make_async_copy(
            res_ref.at[:, pl.ds(pl.multiple_of(e * COLS, COLS), COLS)], res, ld.at[2]
        ),
        pltpu.make_async_copy(wg_ref.at[0], wg.at[0:FF], ld.at[3]),
        pltpu.make_async_copy(wu_ref.at[0], wu.at[0:FF], ld.at[4]),
        pltpu.make_async_copy(wd_ref.at[0], wd.at[0:FF], ld.at[5]),
    ]

    def kv_rows(kk, bb, aa, units=1):
        return pl.ds(pl.multiple_of((kk * NB + bb * 4 + aa) * TOK, TOK), units * TOK)

    own = kv_rows(core, b, a)
    own_k = pltpu.make_async_copy(k_ref, kv.at[own, 0:HEAD], ld.at[6])
    own_v = pltpu.make_async_copy(v_ref, kv.at[own, HEAD : 2 * HEAD], ld.at[7])

    steps = [(da, db) for db in (0, 1, 3, 2) for da in (0, 1, 3, 2) if da + db > 0]

    def at_step(da, db):
        return lax.rem(a + da, 4), lax.rem(b + db, 4)

    own_k.start()
    own_v.start()
    barrier = pltpu.get_barrier_semaphore()
    for da, db in steps:
        pl.semaphore_signal(
            barrier, inc=1, device_id=(ctx_of(*at_step(da, db)), e), device_id_type=MESH
        )
    for s in range(1, NZ):
        pl.semaphore_signal(barrier, inc=1, device_id=to_z(s), device_id_type=MESH)
    pl.semaphore_signal(barrier, inc=1, device_id=to_sib, device_id_type=MESH)
    loads[0].start()
    own_k.wait()
    own_v.wait()
    pl.semaphore_wait(barrier, len(steps) + NZ)

    mine_kv = kv.at[own, :]
    for i, (da, db) in enumerate(steps):
        device = (ctx_of(*at_step(da, db)), e)
        remote(mine_kv, mine_kv, kvs.at[i], kvr.at[db * 4 + da], device).start()
    for copy in loads[1:]:
        copy.start()

    ids = ids_ref[...]
    first_id, second_id = ids[0:1, :], ids[1:2, :]
    number = iota((NZ, TOK), 0)
    named = jnp.where((first_id == number) | (second_id == number), 1.0, 0.0)
    before = jnp.where(iota((TOK, TOK), 0) < iota((TOK, TOK), 1), 1.0, 0.0).astype(BF16)
    slot = jnp.dot(named.astype(BF16), before, preferred_element_type=F32)
    slot = jnp.where(named > 0.0, slot, -1.0)
    row = iota((2 * MAIN, TOK), 0)
    wanted = jnp.where(row < MAIN, row, MAIN + lax.rem(row, REM)).astype(F32)
    for k in range(NZ):
        here = jnp.broadcast_to(slot[k : k + 1, :], (2 * MAIN, TOK)) == wanted
        place[k * 2 * MAIN : (k + 1) * 2 * MAIN, :] = jnp.where(here, 1.0, 0.0).astype(BF16)
    my_slot = jnp.sum(jnp.where(number == e, slot, 0.0), axis=0, keepdims=True)
    by_token = jnp.where(
        jnp.broadcast_to(my_slot, (HEAD, TOK)) == iota((HEAD, TOK), 0).astype(F32), 1.0, 0.0
    ).astype(BF16)
    eye = jnp.where(iota((TOK, TOK), 0) == iota((TOK, TOK), 1), 1.0, 0.0)
    slot_of_token = lax.dot_general(eye.astype(BF16), by_token, NT, preferred_element_type=F32)

    r256, l256 = iota((256, 256), 0), iota((256, 256), 1)
    i64 = lax.rem(r256, 64)
    to_unit = lax.div(i64, REM) * 16 + lax.div(r256, 64) * REM + lax.rem(i64, REM)
    perm[...] = jnp.where(l256 == to_unit, 1.0, 0.0).astype(BF16)
    to_flat = lax.rem(lax.div(r256, REM), 4) * 64 + lax.div(r256, 16) * REM + lax.rem(r256, REM)
    unperm[...] = jnp.where(l256 == to_flat, 1.0, 0.0).astype(BF16)

    gate_acc[...] = jnp.zeros_like(gate_acc)
    up_acc[...] = jnp.zeros_like(up_acc)
    half = COLS // 2
    stats[e] = jnp.zeros((2 * NZ, 128), F32)
    top[...] = jnp.full(top.shape, -1e30, F32)
    tot[...] = jnp.zeros_like(tot)
    acc[...] = jnp.zeros_like(acc)

    loads[0].wait()
    for g in range(GROUPS):
        qs[g * TOK : (g + 1) * TOK, :] = qv[:, g * HEAD : (g + 1) * HEAD]

    klane, vlane = slice(0, HEAD), slice(HEAD, 2 * HEAD)

    def row_wait(db, bb):
        for da in range(4):
            if da + db > 0:
                wait(kv.at[kv_rows(core, bb, lax.rem(a + 4 - da, 4)), :], kvr.at[db * 4 + da])

    def row_pass(i, bb):
        rows = kv.at[kv_rows(core, bb, 0, 4), :]
        remote(rows, rows, kvs.at[15 + i], kvr.at[16 + i], to_sib).start()

    query_pos = c * TOK + lax.rem(iota((GROUPS * TOK, 1), 0), TOK)
    lane = iota((1, BUNDLE), 1)
    score_scale = 1.0 / math.sqrt(HEAD)

    def attend(kk, bb):
        rows = kv_rows(kk, bb, 0, 4)
        key_pos = (
            TOK * kk
            + lax.rem(lane, TOK)
            + 2 * TOK * ((1 + 3 * kk) * lax.div(lane, TOK) + (4 - 3 * kk) * bb)
        )
        scores = (
            lax.dot_general(qs[...], kv[rows, klane], NT, preferred_element_type=F32) * score_scale
        )
        allowed = key_pos <= query_pos
        if SEQ > WINDOW:
            allowed = allowed & (key_pos > query_pos - WINDOW)
        scores = jnp.where(allowed, scores, -1e30)
        old = top[:, 0:1]
        new = jnp.maximum(old, jnp.max(scores, axis=1, keepdims=True))
        fade = jnp.exp(old - new)
        weights = jnp.exp(scores - new)
        top[...] = jnp.broadcast_to(new, top.shape)
        tot[...] = tot[...] * fade + jnp.sum(weights, axis=1, keepdims=True)
        acc[...] = acc[...] * fade + jnp.dot(
            weights.astype(BF16), kv[rows, vlane], preferred_element_type=F32
        )

    def other_wait(i, aa):
        wait(kv.at[kv_rows(1 - core, aa, 0, 4), :], kvr.at[16 + i])

    row_wait(0, b)
    row_pass(0, b)
    attend(core, b)
    other_wait(0, a)
    attend(1 - core, a)
    row_wait(1, bm)
    row_pass(1, bm)
    row_wait(3, bp)
    row_pass(2, bp)
    attend(core, bm)
    attend(core, bp)
    row_wait(2, b2)
    row_pass(3, b2)
    for i, (src, dst) in enumerate(((wg_ref, wg), (wu_ref, wu), (wd_ref, wd))):
        remote(src.at[0], dst.at[FF : 2 * FF], ws.at[i], wr.at[i], to_sib).start()
    other_wait(1, am)
    attend(1 - core, am)
    other_wait(2, ap)
    attend(1 - core, ap)
    attend(core, b2)
    other_wait(3, a2)
    attend(1 - core, a2)

    for g in range(GROUPS):
        rows = slice(g * TOK, (g + 1) * TOK)
        attn[:, g * HEAD : (g + 1) * HEAD] = (acc[rows, :] / tot[rows, 0:1]).astype(BF16)

    def cols(j):
        return pl.ds(pl.multiple_of(j * COLS, COLS), COLS)

    def project(s):
        return jnp.dot(attn[...], wo[:, cols(chunk(s))], preferred_element_type=F32)

    lo, hi = slice(0, half), slice(half, COLS)
    full = slice(0, COLS)
    moves = (
        (0, lo, 0, 2), (0, hi, 7, -2), (1, full, 1, 1), (2, full, 2, -1), (3, full, 3, 1), (4, full, 4, -1),
        (5, full, 5, 2), (6, full, 6, -2),
    )

    def sum_send(k):
        i, lanes, sem, step = moves[k]
        remote(
            zs.at[i, :, lanes], zr.at[i, :, lanes], z1s.at[sem], z1r.at[sem], to_z(step)
        ).start()

    def sum_wait(k):
        i, lanes, sem, _ = moves[k]
        wait(zr.at[i, :, lanes], z1r.at[sem])

    loads[1].wait()
    zs[0] = project(4).astype(BF16)
    sum_send(0)
    sum_send(1)
    for i, s in ((1, 3), (2, -3), (3, 1), (4, -1)):
        zs[i] = project(s).astype(BF16)
        sum_send(i + 1)
    up, down = project(2), project(-2)
    loads[2].wait()
    total = project(0) + res[...].astype(F32)
    sum_wait(2)
    sum_wait(0)
    up = up + zr[1].astype(F32)
    zs[5, :, lo] = (up[:, lo] + zr[0, :, lo].astype(F32)).astype(BF16)
    zs[5, :, hi] = up[:, hi].astype(BF16)
    sum_send(6)
    sum_wait(3)
    sum_wait(1)
    down = down + zr[2].astype(F32)
    zs[6, :, hi] = (down[:, hi] + zr[0, :, hi].astype(F32)).astype(BF16)
    zs[6, :, lo] = down[:, lo].astype(BF16)
    sum_send(7)
    sum_wait(4)
    sum_wait(5)
    total = total + zr[3].astype(F32) + zr[4].astype(F32)
    sum_wait(6)
    sum_wait(7)
    total = (total + zr[5].astype(F32) + zr[6].astype(F32)).astype(BF16)
    att[e] = total

    def unit(aa, bb):
        return pl.ds(pl.multiple_of((bb * 4 + aa) * MAIN, MAIN), MAIN)

    tile = lax.div(iota((MAIN, 128), 0), REM)
    value = total.astype(F32)
    scaled = (value * gain_ref[:, cols(e)]).astype(BF16)
    packed = jnp.dot(place[...], scaled, preferred_element_type=F32)
    for k in range(NZ):
        at = k * 2 * MAIN
        zunits[k, :, 0:COLS] = packed[at : at + MAIN].astype(BF16)
        rest = jnp.zeros((MAIN, 128), F32)
        for t in range(4):
            rest = rest + jnp.where(
                tile == t, packed[at + MAIN : at + 2 * MAIN, t * 128 : (t + 1) * 128], 0.0
            )
        zunits[k, :, COLS:UNIT] = rest.astype(BF16)
    spread_steps = ((1, 2), (-1, 1), (2, 4), (-2, 3), (3, 6), (-3, 5), (4, 7))
    for s, n in spread_steps:
        remote(
            zunits.at[chunk(s)], slots.at[e, unit(a, b), :], zas.at[n], zar.at[n], to_z(s)
        ).start()
    slots[e, unit(a, b), :] = zunits[e]
    squares = jnp.sum(value * value, axis=1, keepdims=True)
    stats[e, 0:NZ, 0:TOK] = lax.dot_general(
        rt_ref[:, cols(e)], scaled, NT, preferred_element_type=F32
    )
    stats[e, NZ : 2 * NZ, 0:TOK] = jnp.broadcast_to(
        jnp.sum(eye * squares, axis=0, keepdims=True), (NZ, TOK)
    )

    def ag_chunk(n):
        odd = lax.rem(n, 2)
        return chunk((2 * odd - 1) * lax.div(n + 1, 2))

    def bundle(bb):
        return pl.ds(pl.multiple_of(bb * 64, 64), 64)

    def first_half(bb):
        return pl.ds(pl.multiple_of(bb * 64, 32), 32)

    def second_half(bb):
        return pl.ds(pl.multiple_of(bb * 64 + 32, 32), 32)

    def scale_unit(aa, bb):
        return pl.ds(pl.multiple_of((bb * 4 + aa) * 8, 8), 8)

    def scale_bundle(bb):
        return pl.ds(pl.multiple_of(bb * 32, 8), 32)

    def out_copy(j):
        return pltpu.make_async_copy(att.at[j], att_out.at[:, cols(j)], outs.at[j])

    def token_stats():
        whole = stats[0]
        for k in range(1, NZ):
            whole = whole + stats[k]
        inverse = lax.rsqrt(whole[NZ : NZ + 1, 0:TOK] * (1.0 / D) + 1e-05)
        return whole[0:NZ, 0:TOK] * inverse, inverse

    def ag_start(n):
        j = ag_chunk(n)
        here = slots.at[j, unit(a, b), :]

        @pl.when(n > 0)
        def _():
            wait(here, zar.at[n])

        remote(here, here, ags.at[0, n], agr.at[0, n], to_ap).start()
        remote(here, here, ags.at[1, n], agr.at[1, n], to_am).start()
        remote(here, here, ags.at[2, n], agr.at[2, n], to_a2).start()

        @pl.when(n == 0)
        def _():
            for s, k in spread_steps:
                remote(stats.at[e], stats.at[e], sts.at[k], str_.at[k], to_z(s)).start()
            for s, k in spread_steps:
                remote(att.at[e], att.at[e], ats.at[k], atr.at[k], to_z(s)).start()

        @pl.when(n == 7)
        def _():
            for k in range(1, NZ):
                wait(stats.at[ag_chunk(k)], str_.at[k])
            inverse = token_stats()[1]
            inverse = jnp.sum(eye * inverse, axis=1, keepdims=True)
            by_slot = jnp.sum(slot_of_token * inverse, axis=0, keepdims=True)
            scales[scale_unit(a, b), :] = jnp.broadcast_to(by_slot, (8, HEAD))
            here = scales.at[scale_unit(a, b), :]
            remote(here, here, scs.at[0], scr.at[0], to_ap).start()
            remote(here, here, scs.at[1], scr.at[1], to_am).start()
            remote(here, here, scs.at[2], scr.at[2], to_a2).start()

    def ag_second(n):
        j = ag_chunk(n)
        wait(slots.at[j, unit(am, b), :], agr.at[0, n])
        wait(slots.at[j, unit(ap, b), :], agr.at[1, n])
        wait(slots.at[j, unit(a2, b), :], agr.at[2, n])
        piece = slots.at[j, bundle(b), :]
        remote(piece, piece, ags.at[3, n], agr.at[3, n], to_bp).start()
        remote(piece, piece, ags.at[4, n], agr.at[4, n], to_bm).start()

        @pl.when(n >= AG_RELAYED)
        def _():
            remote(piece, piece, ags.at[5, n], agr.at[5, n], to_b2).start()

        @pl.when(n == 7)
        def _():
            wait(scales.at[scale_unit(am, b), :], scr.at[0])
            wait(scales.at[scale_unit(ap, b), :], scr.at[1])
            wait(scales.at[scale_unit(a2, b), :], scr.at[2])
            piece = scales.at[scale_bundle(b), :]
            remote(piece, piece, scs.at[3], scr.at[3], to_bp).start()
            remote(piece, piece, scs.at[4], scr.at[4], to_bm).start()
            remote(piece, piece, scs.at[5], scr.at[5], to_b2).start()

    def ag_third(n):
        j = ag_chunk(n)

        @pl.when(n < AG_RELAYED)
        def _():
            wait(slots.at[j, bundle(bm), :], agr.at[3, n])
            piece = slots.at[j, first_half(bm), :]
            remote(piece, piece, ags.at[5, n], agr.at[5, n], to_bp).start()
            wait(slots.at[j, bundle(bp), :], agr.at[4, n])
            piece = slots.at[j, second_half(bp), :]
            remote(piece, piece, ags.at[6, n], agr.at[6, n], to_bm).start()

    def ag_use(n):
        j = ag_chunk(n)

        @pl.when(n < AG_RELAYED)
        def _():
            wait(slots.at[j, first_half(b2), :], agr.at[5, n])
            wait(slots.at[j, second_half(b2), :], agr.at[6, n])

        @pl.when(n >= AG_RELAYED)
        def _():
            wait(slots.at[j, bundle(bm), :], agr.at[3, n])
            wait(slots.at[j, bundle(bp), :], agr.at[4, n])
            wait(slots.at[j, bundle(b2), :], agr.at[5, n])

        flat = jnp.dot(
            perm[...], slots[j, 0:256, COLS:UNIT], preferred_element_type=F32
        ).astype(BF16)
        for t in range(4):
            slots[j, 256:ROWS, t * 128 : (t + 1) * 128] = flat[t * 64 : (t + 1) * 64]
        rows = slots[j, :, 0:COLS]
        gate_acc[...] += lax.dot_general(rows, wg[:, cols(j)], NT, preferred_element_type=F32)
        up_acc[...] += lax.dot_general(rows, wu[:, cols(j)], NT, preferred_element_type=F32)

    def run(stages, count):
        last = max(lag for _, lag in stages)

        def tick(t, carry):
            for function, lag in stages:

                @pl.when((t >= lag) & (t < lag + count))
                def _(function=function, lag=lag):
                    function(t - lag)

            return carry

        lax.fori_loop(0, count + last, tick, 0)

    loads[3].wait()
    loads[4].wait()
    wait(wg.at[FF : 2 * FF], wr.at[0])
    wait(wu.at[FF : 2 * FF], wr.at[1])
    run(((ag_third, AG_LAGS[1]), (ag_second, AG_LAGS[0]), (ag_start, 0), (ag_use, AG_LAGS[2])), NZ)
    wait(scales.at[scale_bundle(bm), :], scr.at[3])
    wait(scales.at[scale_bundle(bp), :], scr.at[4])
    wait(scales.at[scale_bundle(b2), :], scr.at[5])

    row = iota((ROWS, HEAD), 0)
    col = iota((ROWS, HEAD), 1)
    over = row - 256
    block_of = jnp.where(row < 256, lax.div(row, MAIN), lax.div(over, REM))
    slot_of = jnp.where(row < 256, lax.rem(row, MAIN), MAIN + lax.rem(over + 256, REM))
    pick = jnp.where(col == block_of * 8, 1.0, 0.0)
    spread = jnp.dot(pick, scales[...], precision=HIGH, preferred_element_type=F32)
    factor = jnp.sum(jnp.where(col == slot_of, spread, 0.0), axis=1, keepdims=True)
    gated = gate_acc[...] * factor
    hid[...] = (gated / (1.0 + jnp.exp(-gated)) * (up_acc[...] * factor)).astype(BF16)
    loads[5].wait()
    wait(wd.at[FF : 2 * FF], wr.at[2])

    def rs_chunk(n):
        odd = lax.rem(n, 2)
        return chunk(odd * (4 - lax.div(n + 1, 2)) - (1 - odd) * (4 - lax.div(n, 2)))

    def rs_start(n):
        j = rs_chunk(n)
        out = jnp.dot(hid[...], wd[:, cols(j)], preferred_element_type=F32).astype(BF16)
        part[n, :, 0:COLS] = out[0:256]
        rest = jnp.concatenate([out[256:, t * 128 : (t + 1) * 128] for t in range(4)], axis=0)
        part[n, :, COLS:UNIT] = jnp.dot(unperm[...], rest, preferred_element_type=F32).astype(BF16)

        @pl.when(n < RS_RELAYED)
        def _():
            remote(
                part.at[n, first_half(b2), :], r1p.at[n], rss.at[0, n], rsr.at[0, n], to_bp
            ).start()
            remote(
                part.at[n, second_half(b2), :], r1m.at[n], rss.at[1, n], rsr.at[1, n], to_bm
            ).start()

        @pl.when(n >= RS_RELAYED)
        def _():
            remote(part.at[n, bundle(b2), :], r2x.at[n], rss.at[0, n], rsr.at[0, n], to_b2).start()
            remote(part.at[n, bundle(bp), :], r2p.at[n], rss.at[2, n], rsr.at[2, n], to_bp).start()
            remote(part.at[n, bundle(bm), :], r2m.at[n], rss.at[3, n], rsr.at[3, n], to_bm).start()

        @pl.when(n > 0)
        def _():
            wait(att.at[ag_chunk(n)], atr.at[n])

        out_copy(ag_chunk(n)).start()

        @pl.when(n == 7)
        def _():
            logits = token_stats()[0]
            one = jnp.sum(jnp.where(number == first_id, logits, 0.0), axis=0, keepdims=True)
            two = jnp.sum(jnp.where(number == second_id, logits, 0.0), axis=0, keepdims=True)
            gate = 1.0 / (1.0 + jnp.exp(two - one))
            gates = jnp.where(first_id == number, gate, 1.0 - gate)
            spread = jnp.concatenate(
                [jnp.broadcast_to(gates[k : k + 1, :], (2 * MAIN, TOK)) for k in range(NZ)], axis=0
            )
            spread = spread * place[...].astype(F32)
            turned = lax.dot_general(eye, spread, NT, precision=HIGH, preferred_element_type=F32)
            high = turned.astype(BF16)
            wgt_hi[...] = high
            wgt_lo[...] = (turned - high.astype(F32)).astype(BF16)

    def add(n, rows, lanes, more):
        value = part[n, rows, lanes].astype(F32)
        for term in more:
            value = value + term.astype(F32)
        return value

    every = slice(0, UNIT)

    def rs_first(n):
        @pl.when(n < RS_RELAYED)
        def _():
            wait(r1p.at[n], rsr.at[0, n])
            rows = first_half(bp)
            part[n, rows, every] = add(n, rows, every, [r1p[n]]).astype(BF16)
            remote(part.at[n, bundle(bp), :], r2p.at[n], rss.at[2, n], rsr.at[2, n], to_bp).start()
            wait(r1m.at[n], rsr.at[1, n])
            rows = second_half(bm)
            part[n, rows, every] = add(n, rows, every, [r1m[n]]).astype(BF16)
            remote(part.at[n, bundle(bm), :], r2m.at[n], rss.at[3, n], rsr.at[3, n], to_bm).start()

    def rs_second(n):
        wait(r2p.at[n], rsr.at[2, n])
        wait(r2m.at[n], rsr.at[3, n])
        rows = bundle(b)

        @pl.when(n < RS_RELAYED)
        def _():
            part[n, rows, every] = add(n, rows, every, [r2p[n], r2m[n]]).astype(BF16)

        @pl.when(n >= RS_RELAYED)
        def _():
            wait(r2x.at[n], rsr.at[0, n])
            part[n, rows, every] = add(n, rows, every, [r2p[n], r2m[n], r2x[n]]).astype(BF16)

        remote(part.at[n, unit(a2, b), :], r4x.at[n], rss.at[4, n], rsr.at[4, n], to_a2).start()
        remote(part.at[n, unit(ap, b), :], r4p.at[n], rss.at[5, n], rsr.at[5, n], to_ap).start()
        remote(part.at[n, unit(am, b), :], r4m.at[n], rss.at[6, n], rsr.at[6, n], to_am).start()

    def rs_last(n):
        wait(r4p.at[n], rsr.at[5, n])
        wait(r4m.at[n], rsr.at[6, n])
        wait(r4x.at[n], rsr.at[4, n])
        zout[n] = add(n, unit(a, b), every, [r4p[n], r4m[n], r4x[n]]).astype(BF16)

        @pl.when(n < 7)
        def _():
            remote(zout.at[n], fin.at[e], z2s.at[n], z2r.at[7 - n], (c, rs_chunk(n))).start()

        @pl.when(n == 7)
        def _():
            fin[e] = zout[7]

    run(((rs_last, RS_LAGS[2]), (rs_second, RS_LAGS[1]), (rs_first, RS_LAGS[0]), (rs_start, 0)), NZ)

    for n in range(1, NZ):
        wait(fin.at[ag_chunk(n)], z2r.at[n])
    for k in range(NZ):
        at = k * 2 * MAIN
        terms[at : at + MAIN, :] = fin[k, :, 0:COLS]
        rest = fin[k, :, COLS:UNIT].astype(F32)
        for t in range(4):
            terms[at + MAIN : at + 2 * MAIN, t * 128 : (t + 1) * 128] = jnp.where(
                tile == t, rest, 0.0
            ).astype(BF16)
    mixed = jnp.dot(wgt_hi[...], terms[...], preferred_element_type=F32)
    mixed = mixed + jnp.dot(wgt_lo[...], terms[...], preferred_element_type=F32)
    mix_out[...] = mixed.astype(BF16)

    for i in range(15):
        wait(mine_kv, kvs.at[i])
    for i in range(4):
        wait(kv.at[0 : 4 * TOK, :], kvs.at[15 + i])
    for i, ref in enumerate((wg, wu, wd)):
        wait(ref.at[FF : 2 * FF], ws.at[i])
    for i, lanes, sem, _ in moves:
        wait(zs.at[i, :, lanes], z1s.at[sem])

    def drain(n, carry):
        for i, rows in enumerate((MAIN, MAIN, MAIN, 64, 64)):
            wait(slots.at[0, 0:rows, :], ags.at[i, n])

        @pl.when(n < AG_RELAYED)
        def _():
            wait(slots.at[0, 0:32, :], ags.at[5, n])
            wait(slots.at[0, 0:32, :], ags.at[6, n])

        @pl.when(n >= AG_RELAYED)
        def _():
            wait(slots.at[0, 0:64, :], ags.at[5, n])

        @pl.when(n < RS_RELAYED)
        def _():
            wait(r1p.at[0], rss.at[0, n])
            wait(r1p.at[0], rss.at[1, n])

        @pl.when(n >= RS_RELAYED)
        def _():
            wait(r2x.at[0], rss.at[0, n])

        for i, piece in ((2, r2p), (3, r2m), (4, r4x), (5, r4p), (6, r4m)):
            wait(piece.at[0], rss.at[i, n])

        @pl.when(n < 7)
        def _():
            wait(zout.at[0], z2s.at[n])
            wait(zunits.at[0], zas.at[n + 1])
            wait(stats.at[0], sts.at[n + 1])
            wait(att.at[0], ats.at[n + 1])

        out_copy(n).wait()
        return carry

    lax.fori_loop(0, NZ, drain, 0)
    for i in range(6):
        wait(scales.at[0:8, :] if i < 3 else scales.at[0:32, :], scs.at[i])


def local(
    query, key_states, value_states, residual, out_weight, norm_gain, router_weight, expert_ids,
    gate_weight, up_weight, down_weight,
):
    anywhere = pl.BlockSpec(memory_space=pl.ANY)
    near = pl.BlockSpec(memory_space=pltpu.VMEM)
    vmem = pltpu.VMEM
    dma = pltpu.SemaphoreType.DMA
    scratch = [
        vmem((TOK, GROUPS * HEAD), BF16),
        vmem((SEQ, 2 * HEAD), BF16),
        vmem((GROUPS * TOK, HEAD), BF16),
        vmem((GROUPS * TOK, HEAD), F32),
        vmem((GROUPS * TOK, HEAD), F32),
        vmem((GROUPS * TOK, HEAD), F32),
        vmem((TOK, GROUPS * HEAD), BF16),
        vmem((GROUPS * HEAD, D), BF16),
        vmem((TOK, COLS), BF16),
        vmem((2 * FF, D), BF16),
        vmem((2 * FF, D), BF16),
        vmem((2 * FF, D), BF16),
        vmem((7, TOK, COLS), BF16),
        vmem((7, TOK, COLS), BF16),
        vmem((NZ, TOK, COLS), BF16),
        vmem((NZ, 2 * NZ, 128), F32),
        vmem((NZ * 2 * MAIN, TOK), BF16),
        vmem((256, 256), BF16),
        vmem((256, 256), BF16),
        vmem((NZ, MAIN, UNIT), BF16),
        vmem((NZ, ROWS, UNIT), BF16),
        vmem((NB * 8, HEAD), F32),
        vmem((ROWS, 2 * FF), F32),
        vmem((ROWS, 2 * FF), F32),
        vmem((ROWS, 2 * FF), BF16),
        vmem((TOK, NZ * 2 * MAIN), BF16),
        vmem((TOK, NZ * 2 * MAIN), BF16),
        vmem((NZ, 256, UNIT), BF16),
        vmem((NZ, 32, UNIT), BF16),
        vmem((NZ, 32, UNIT), BF16),
        vmem((NZ, 64, UNIT), BF16),
        vmem((NZ, 64, UNIT), BF16),
        vmem((NZ, 64, UNIT), BF16),
        vmem((NZ, MAIN, UNIT), BF16),
        vmem((NZ, MAIN, UNIT), BF16),
        vmem((NZ, MAIN, UNIT), BF16),
        vmem((NZ, MAIN, UNIT), BF16),
        vmem((NZ, MAIN, UNIT), BF16),
        vmem((NZ * 2 * MAIN, COLS), BF16),
        dma((8,)),
        dma((19,)),
        dma((20,)),
        dma((3,)),
        dma((3,)),
        dma((8,)),
        dma((8,)),
        dma((8,)),
        dma((8,)),
        dma((8,)),
        dma((8,)),
        dma((8,)),
        dma((8,)),
        dma((7, NZ)),
        dma((7, NZ)),
        dma((6,)),
        dma((6,)),
        dma((7, NZ)),
        dma((7, NZ)),
        dma((8,)),
        dma((8,)),
        dma((NZ,)),
    ]
    return pl.pallas_call(
        kernel,
        out_shape=(
            jax.ShapeDtypeStruct((TOK, D), BF16),
            jax.ShapeDtypeStruct((TOK, COLS), BF16),
        ),
        in_specs=[anywhere] * 5 + [near] * 3 + [anywhere] * 3,
        out_specs=(anywhere, near),
        scratch_shapes=scratch,
        compiler_params=pltpu.CompilerParams(
            collective_id=0, has_side_effects=True, vmem_limit_bytes=56 * 1024 * 1024
        ),
        name="layer",
    )(
        query,
        key_states,
        value_states,
        residual,
        out_weight,
        norm_gain.reshape(1, D),
        router_weight.T,
        expert_ids.T,
        jnp.swapaxes(gate_weight, 1, 2),
        jnp.swapaxes(up_weight, 1, 2),
        down_weight,
    )


def solution(mesh):
    placed = (
        P("ctx", "exp"),
        P("ctx", "exp"),
        P("ctx", "exp"),
        P("ctx", None),
        P("exp", None),
        P(),
        P(),
        P("ctx", None),
        P("exp", None, "ctx"),
        P("exp", None, "ctx"),
        P("exp", "ctx", None),
    )
    return jax.shard_map(
        local,
        mesh=mesh,
        in_specs=placed,
        out_specs=(P("ctx", None), P("ctx", "exp")),
        check_vma=False,
    )
```

```python
import functools
import math

import jax
import jax.numpy as jnp
from jax import lax
from jax.experimental import pallas as pl
from jax.experimental.pallas import tpu as pltpu
from jax.sharding import PartitionSpec as P

WINDOW = 4096
SEQ = 2048
D = 4096
TOK = 64
CAP = 20
FF = 224
NZ = 8
COLS = D // NZ
HEAD = 128
GROUPS = 4
NB = 16
MAIN = 16
REM = CAP - MAIN
UNIT = COLS + 128
BUNDLE = 4 * TOK
ROWS = NB * CAP
F32 = jnp.float32
BF16 = jnp.bfloat16
MESH = pl.DeviceIdType.MESH
HIGH = lax.Precision.HIGHEST
NT = (((1,), (1,)), ((), ()))

RS_LAGS = (3, 6, 9)
AG_RELAYED = 8
RS_RELAYED = 8


def iota(shape, dim):
    return lax.broadcasted_iota(jnp.int32, shape, dim)


def remote(src, dst, send, recv, device):
    return pltpu.make_async_remote_copy(
        src_ref=src, dst_ref=dst, send_sem=send, recv_sem=recv, device_id=device, device_id_type=MESH
    )


def wait(ref, sem):
    pltpu.make_async_copy(ref, ref, sem).wait()


def kernel(
    q_ref, k_ref, v_ref, res_ref, wo_ref, gain_hbm, rt_hbm, ids_hbm, wg_ref, wu_ref, wd_ref,
    att_out, mix_out,
    gain_ref, rt_ref, ids_ref, mixed_out, qv, kv, qs, top, tot, acc, attn, wo, res, wg, wu, wd,
    zs, zr, att, stats, place, perm, unperm, zunits,
    slots, scales, gate_acc, up_acc, hid, wgt_hi, wgt_lo,
    part, r1p, r1m, r2p, r2m, r2x, r4p, r4m, r4x, zout, fin, terms,
    ld, kvs, kvr, ws, wr, z1s, z1r, zas, zar, dis, dir_, sts, str_, ats, atr, ags, agr, scs, scr, rss, rsr,
    z2s, z2r, outs,
):
    c = lax.axis_index("ctx")
    e = lax.axis_index("exp")
    core = lax.rem(c, 2)
    chip = lax.div(c, 2)
    x = lax.rem(chip, 4)
    y = lax.div(chip, 4)
    a = x + core * (y - x)
    b = y + core * (x - y)

    def ctx_of(aa, bb):
        return ((bb + core * (aa - bb)) * 4 + aa + core * (bb - aa)) * 2 + core

    ap, am, a2 = lax.rem(a + 1, 4), lax.rem(a + 3, 4), lax.rem(a + 2, 4)
    bp, bm, b2 = lax.rem(b + 1, 4), lax.rem(b + 3, 4), lax.rem(b + 2, 4)
    to_ap, to_am, to_a2 = (ctx_of(ap, b), e), (ctx_of(am, b), e), (ctx_of(a2, b), e)
    to_bp, to_bm, to_b2 = (ctx_of(a, bp), e), (ctx_of(a, bm), e), (ctx_of(a, b2), e)

    def chunk(s):
        return lax.rem(e + s + NZ, NZ)

    def to_z(s):
        return (c, chunk(s))

    to_sib = (c + 1 - 2 * core, e)

    loads = [
        pltpu.make_async_copy(q_ref, qv, ld.at[0]),
        pltpu.make_async_copy(wo_ref, wo, ld.at[1]),
        pltpu.make_async_copy(
            res_ref.at[:, pl.ds(pl.multiple_of(e * COLS, COLS), COLS)], res, ld.at[2]
        ),
        pltpu.make_async_copy(wg_ref.at[0], wg.at[0:FF], ld.at[3]),
        pltpu.make_async_copy(wu_ref.at[0], wu.at[0:FF], ld.at[4]),
        pltpu.make_async_copy(wd_ref.at[0], wd.at[0:FF], ld.at[5]),
        pltpu.make_async_copy(gain_hbm, gain_ref, ld.at[8]),
        pltpu.make_async_copy(rt_hbm, rt_ref, ld.at[9]),
    ]

    def kv_rows(kk, bb, aa, units=1):
        return pl.ds(pl.multiple_of((kk * NB + bb * 4 + aa) * TOK, TOK), units * TOK)

    own = kv_rows(core, b, a)
    own_k = pltpu.make_async_copy(k_ref, kv.at[own, 0:HEAD], ld.at[6])
    own_v = pltpu.make_async_copy(v_ref, kv.at[own, HEAD : 2 * HEAD], ld.at[7])

    steps = [(da, db) for db in (0, 1, 3, 2) for da in (0, 1, 3, 2) if da + db > 0]

    def at_step(da, db):
        return lax.rem(a + da, 4), lax.rem(b + db, 4)

    own_ids = pltpu.make_async_copy(ids_hbm, ids_ref, ld.at[10])
    own_k.start()
    own_v.start()
    barrier = pltpu.get_barrier_semaphore()
    for da, db in steps:
        pl.semaphore_signal(
            barrier, inc=1, device_id=(ctx_of(*at_step(da, db)), e), device_id_type=MESH
        )
    for s in range(1, NZ):
        pl.semaphore_signal(barrier, inc=1, device_id=to_z(s), device_id_type=MESH)
    pl.semaphore_signal(barrier, inc=1, device_id=to_sib, device_id_type=MESH)
    for s in (1, -1):
        for da in (1, 2, 3):
            other = (ctx_of(*at_step(da, 0)), chunk(s))
            pl.semaphore_signal(barrier, inc=1, device_id=other, device_id_type=MESH)
    loads[0].start()
    own_ids.start()
    own_k.wait()
    own_v.wait()
    pl.semaphore_wait(barrier, len(steps) + NZ + 6)

    mine_kv = kv.at[own, :]
    for i, (da, db) in enumerate(steps):
        device = (ctx_of(*at_step(da, db)), e)
        remote(mine_kv, mine_kv, kvs.at[i], kvr.at[db * 4 + da], device).start()
    for copy in loads[1:]:
        copy.start()

    own_ids.wait()
    ids = ids_ref[...]
    first_id, second_id = ids[0:1, :], ids[1:2, :]
    number = iota((NZ, TOK), 0)
    named = jnp.where((first_id == number) | (second_id == number), 1.0, 0.0)
    before = jnp.where(iota((TOK, TOK), 0) < iota((TOK, TOK), 1), 1.0, 0.0).astype(BF16)
    slot = jnp.dot(named.astype(BF16), before, preferred_element_type=F32)
    slot = jnp.where(named > 0.0, slot, -1.0)
    row = iota((2 * MAIN, TOK), 0)
    wanted = jnp.where(row < MAIN, row, MAIN + lax.rem(row, REM)).astype(F32)
    for k in range(NZ):
        here = jnp.broadcast_to(slot[k : k + 1, :], (2 * MAIN, TOK)) == wanted
        place[k * 2 * MAIN : (k + 1) * 2 * MAIN, :] = jnp.where(here, 1.0, 0.0).astype(BF16)
    my_slot = jnp.sum(jnp.where(number == e, slot, 0.0), axis=0, keepdims=True)
    by_token = jnp.where(
        jnp.broadcast_to(my_slot, (HEAD, TOK)) == iota((HEAD, TOK), 0).astype(F32), 1.0, 0.0
    ).astype(BF16)
    eye = jnp.where(iota((TOK, TOK), 0) == iota((TOK, TOK), 1), 1.0, 0.0)
    slot_of_token = lax.dot_general(eye.astype(BF16), by_token, NT, preferred_element_type=F32)

    r256, l256 = iota((256, 256), 0), iota((256, 256), 1)
    i64 = lax.rem(r256, 64)
    to_unit = lax.div(i64, REM) * 16 + lax.div(r256, 64) * REM + lax.rem(i64, REM)
    perm[...] = jnp.where(l256 == to_unit, 1.0, 0.0).astype(BF16)
    to_flat = lax.rem(lax.div(r256, REM), 4) * 64 + lax.div(r256, 16) * REM + lax.rem(r256, REM)
    unperm[...] = jnp.where(l256 == to_flat, 1.0, 0.0).astype(BF16)

    gate_acc[...] = jnp.zeros_like(gate_acc)
    up_acc[...] = jnp.zeros_like(up_acc)
    half = COLS // 2
    stats[e] = jnp.zeros((2 * NZ, 128), F32)
    top[...] = jnp.full(top.shape, -1e30, F32)
    tot[...] = jnp.zeros_like(tot)
    acc[...] = jnp.zeros_like(acc)

    loads[0].wait()
    for g in range(GROUPS):
        qs[g * TOK : (g + 1) * TOK, :] = qv[:, g * HEAD : (g + 1) * HEAD]

    klane, vlane = slice(0, HEAD), slice(HEAD, 2 * HEAD)

    def row_wait(db, bb):
        for da in range(4):
            if da + db > 0:
                wait(kv.at[kv_rows(core, bb, lax.rem(a + 4 - da, 4)), :], kvr.at[db * 4 + da])

    def row_pass(i, bb):
        rows = kv.at[kv_rows(core, bb, 0, 4), :]
        remote(rows, rows, kvs.at[15 + i], kvr.at[16 + i], to_sib).start()

    query_pos = c * TOK + lax.rem(iota((GROUPS * TOK, 1), 0), TOK)
    lane = iota((1, BUNDLE), 1)
    score_scale = 1.0 / math.sqrt(HEAD)

    def attend(kk, bb):
        rows = kv_rows(kk, bb, 0, 4)
        key_pos = (
            TOK * kk
            + lax.rem(lane, TOK)
            + 2 * TOK * ((1 + 3 * kk) * lax.div(lane, TOK) + (4 - 3 * kk) * bb)
        )
        scores = (
            lax.dot_general(qs[...], kv[rows, klane], NT, preferred_element_type=F32) * score_scale
        )
        allowed = key_pos <= query_pos
        if SEQ > WINDOW:
            allowed = allowed & (key_pos > query_pos - WINDOW)
        scores = jnp.where(allowed, scores, -1e30)
        old = top[:, 0:1]
        new = jnp.maximum(old, jnp.max(scores, axis=1, keepdims=True))
        fade = jnp.exp(old - new)
        weights = jnp.exp(scores - new)
        top[...] = jnp.broadcast_to(new, top.shape)
        tot[...] = tot[...] * fade + jnp.sum(weights, axis=1, keepdims=True)
        acc[...] = acc[...] * fade + jnp.dot(
            weights.astype(BF16), kv[rows, vlane], preferred_element_type=F32
        )

    def other_wait(i, aa):
        wait(kv.at[kv_rows(1 - core, aa, 0, 4), :], kvr.at[16 + i])

    row_wait(0, b)
    row_pass(0, b)
    attend(core, b)
    other_wait(0, a)
    attend(1 - core, a)
    row_wait(1, bm)
    row_pass(1, bm)
    row_wait(3, bp)
    row_pass(2, bp)
    attend(core, bm)
    attend(core, bp)
    row_wait(2, b2)
    row_pass(3, b2)
    for i, (src, dst) in enumerate(((wg_ref, wg), (wu_ref, wu), (wd_ref, wd))):
        remote(src.at[0], dst.at[FF : 2 * FF], ws.at[i], wr.at[i], to_sib).start()
    other_wait(1, am)
    attend(1 - core, am)
    other_wait(2, ap)
    attend(1 - core, ap)
    attend(core, b2)
    other_wait(3, a2)
    attend(1 - core, a2)

    for g in range(GROUPS):
        rows = slice(g * TOK, (g + 1) * TOK)
        attn[:, g * HEAD : (g + 1) * HEAD] = (acc[rows, :] / tot[rows, 0:1]).astype(BF16)

    def cols(j):
        return pl.ds(pl.multiple_of(j * COLS, COLS), COLS)

    def project(s):
        return jnp.dot(attn[...], wo[:, cols(chunk(s))], preferred_element_type=F32)

    lo, hi = slice(0, half), slice(half, COLS)
    full = slice(0, COLS)
    moves = (
        (0, lo, 0, 2), (0, hi, 7, -2), (1, full, 1, 1), (2, full, 2, -1), (3, full, 3, 1), (4, full, 4, -1),
        (5, full, 5, 2), (6, full, 6, -2),
    )

    def sum_send(k):
        i, lanes, sem, step = moves[k]
        remote(
            zs.at[i, :, lanes], zr.at[i, :, lanes], z1s.at[sem], z1r.at[sem], to_z(step)
        ).start()

    def sum_wait(k):
        i, lanes, sem, _ = moves[k]
        wait(zr.at[i, :, lanes], z1r.at[sem])

    loads[1].wait()
    zs[0] = project(4).astype(BF16)
    sum_send(0)
    sum_send(1)
    for i, s in ((1, 3), (2, -3), (3, 1), (4, -1)):
        zs[i] = project(s).astype(BF16)
        sum_send(i + 1)
    up, down = project(2), project(-2)
    loads[2].wait()
    total = project(0) + res[...].astype(F32)
    sum_wait(2)
    sum_wait(0)
    up = up + zr[1].astype(F32)
    zs[5, :, lo] = (up[:, lo] + zr[0, :, lo].astype(F32)).astype(BF16)
    zs[5, :, hi] = up[:, hi].astype(BF16)
    sum_send(6)
    sum_wait(3)
    sum_wait(1)
    down = down + zr[2].astype(F32)
    zs[6, :, hi] = (down[:, hi] + zr[0, :, hi].astype(F32)).astype(BF16)
    zs[6, :, lo] = down[:, lo].astype(BF16)
    sum_send(7)
    sum_wait(4)
    sum_wait(5)
    total = total + zr[3].astype(F32) + zr[4].astype(F32)
    sum_wait(6)
    sum_wait(7)
    total = (total + zr[5].astype(F32) + zr[6].astype(F32)).astype(BF16)
    att[e] = total

    loads[6].wait()
    loads[7].wait()
    def unit(aa, bb):
        return pl.ds(pl.multiple_of((bb * 4 + aa) * MAIN, MAIN), MAIN)

    tile = lax.div(iota((MAIN, 128), 0), REM)
    value = total.astype(F32)
    scaled = (value * gain_ref[:, cols(e)]).astype(BF16)
    packed = jnp.dot(place[...], scaled, preferred_element_type=F32)
    for k in range(NZ):
        at = k * 2 * MAIN
        zunits[k, :, 0:COLS] = packed[at : at + MAIN].astype(BF16)
        rest = jnp.zeros((MAIN, 128), F32)
        for t in range(4):
            rest = rest + jnp.where(
                tile == t, packed[at + MAIN : at + 2 * MAIN, t * 128 : (t + 1) * 128], 0.0
            )
        zunits[k, :, COLS:UNIT] = rest.astype(BF16)
    spread_steps = ((1, 2), (-1, 1), (2, 4), (-2, 3), (3, 6), (-3, 5), (4, 7))
    first_steps = ((1, 0), (3, 1), (2, 2))
    mine_rows = unit(a, b)
    for s, n in spread_steps:
        src, dst = zunits.at[chunk(s)], slots.at[e, mine_rows, :]
        remote(src, dst, zas.at[n], zar.at[n], to_z(s)).start()
        if n < 3:
            for da, i in first_steps:
                device = (ctx_of(*at_step(da, 0)), chunk(s))
                remote(src, dst, ags.at[i, n], agr.at[i, n], device).start()
    slots[e, mine_rows, :] = zunits[e]
    for i, (da, db) in enumerate(steps):
        device = (ctx_of(*at_step(da, db)), e)
        here = slots.at[e, mine_rows, :]
        remote(here, here, dis.at[i], dir_.at[db * 4 + da], device).start()
    squares = jnp.sum(value * value, axis=1, keepdims=True)
    stats[e, 0:NZ, 0:TOK] = lax.dot_general(
        rt_ref[:, cols(e)], scaled, NT, preferred_element_type=F32
    )
    stats[e, NZ : 2 * NZ, 0:TOK] = jnp.broadcast_to(
        jnp.sum(eye * squares, axis=0, keepdims=True), (NZ, TOK)
    )

    def ag_chunk(n):
        odd = lax.rem(n, 2)
        return chunk((2 * odd - 1) * lax.div(n + 1, 2))

    def bundle(bb):
        return pl.ds(pl.multiple_of(bb * 64, 64), 64)

    def first_half(bb):
        return pl.ds(pl.multiple_of(bb * 64, 32), 32)

    def second_half(bb):
        return pl.ds(pl.multiple_of(bb * 64 + 32, 32), 32)

    def scale_unit(aa, bb):
        return pl.ds(pl.multiple_of((bb * 4 + aa) * 8, 8), 8)

    def scale_bundle(bb):
        return pl.ds(pl.multiple_of(bb * 32, 8), 32)

    def out_copy(j):
        return pltpu.make_async_copy(att.at[j], att_out.at[:, cols(j)], outs.at[j])

    def token_stats():
        whole = stats[0]
        for k in range(1, NZ):
            whole = whole + stats[k]
        inverse = lax.rsqrt(whole[NZ : NZ + 1, 0:TOK] * (1.0 / D) + 1e-05)
        return whole[0:NZ, 0:TOK] * inverse, inverse

    def stats_send():
        for s, k in spread_steps:
            remote(stats.at[e], stats.at[e], sts.at[k], str_.at[k], to_z(s)).start()

    def columns_send():
        for s, k in spread_steps:
            remote(att.at[e], att.at[e], ats.at[k], atr.at[k], to_z(s)).start()

    def ag_start(n):
        here = slots.at[ag_chunk(n), mine_rows, :]
        wait(here, zar.at[n])
        remote(here, here, ags.at[0, n], agr.at[0, n], to_ap).start()
        remote(here, here, ags.at[1, n], agr.at[1, n], to_am).start()
        remote(here, here, ags.at[2, n], agr.at[2, n], to_a2).start()

    def scale_start():
        for k in range(1, NZ):
            wait(stats.at[ag_chunk(k)], str_.at[k])
        inverse = token_stats()[1]
        inverse = jnp.sum(eye * inverse, axis=1, keepdims=True)
        by_slot = jnp.sum(slot_of_token * inverse, axis=0, keepdims=True)
        scales[scale_unit(a, b), :] = jnp.broadcast_to(by_slot, (8, HEAD))
        here = scales.at[scale_unit(a, b), :]
        remote(here, here, scs.at[0], scr.at[0], to_ap).start()
        remote(here, here, scs.at[1], scr.at[1], to_am).start()
        remote(here, here, scs.at[2], scr.at[2], to_a2).start()

    def scale_second():
        wait(scales.at[scale_unit(am, b), :], scr.at[0])
        wait(scales.at[scale_unit(ap, b), :], scr.at[1])
        wait(scales.at[scale_unit(a2, b), :], scr.at[2])
        piece = scales.at[scale_bundle(b), :]
        remote(piece, piece, scs.at[3], scr.at[3], to_bp).start()
        remote(piece, piece, scs.at[4], scr.at[4], to_bm).start()
        remote(piece, piece, scs.at[5], scr.at[5], to_b2).start()

    def ag_second(n):
        j = ag_chunk(n)
        if isinstance(n, int) and n < 3:
            wait(slots.at[j, mine_rows, :], zar.at[n])
        wait(slots.at[j, unit(am, b), :], agr.at[0, n])
        wait(slots.at[j, unit(ap, b), :], agr.at[1, n])
        wait(slots.at[j, unit(a2, b), :], agr.at[2, n])
        piece = slots.at[j, bundle(b), :]
        remote(piece, piece, ags.at[3, n], agr.at[3, n], to_bp).start()
        remote(piece, piece, ags.at[4, n], agr.at[4, n], to_bm).start()

        @pl.when(n >= AG_RELAYED)
        def _():
            remote(piece, piece, ags.at[5, n], agr.at[5, n], to_b2).start()

    def ag_third(n):
        j = ag_chunk(n)

        wait(slots.at[j, bundle(bm), :], agr.at[3, n])
        piece = slots.at[j, first_half(bm), :]
        remote(piece, piece, ags.at[5, n], agr.at[5, n], to_bp).start()
        wait(slots.at[j, bundle(bp), :], agr.at[4, n])
        piece = slots.at[j, second_half(bp), :]
        remote(piece, piece, ags.at[6, n], agr.at[6, n], to_bm).start()

    def ag_use(n):
        j = ag_chunk(n)

        @pl.when(n == 0)
        def _():
            for da, db in steps:
                rows = unit(lax.rem(a + 4 - da, 4), lax.rem(b + 4 - db, 4))
                wait(slots.at[j, rows, :], dir_.at[db * 4 + da])

        @pl.when((n > 0) & (n < AG_RELAYED))
        def _():
            wait(slots.at[j, first_half(b2), :], agr.at[5, n])
            wait(slots.at[j, second_half(b2), :], agr.at[6, n])

        @pl.when(n >= AG_RELAYED)
        def _():
            wait(slots.at[j, bundle(bm), :], agr.at[3, n])
            wait(slots.at[j, bundle(bp), :], agr.at[4, n])
            wait(slots.at[j, bundle(b2), :], agr.at[5, n])

        flat = jnp.dot(
            perm[...], slots[j, 0:256, COLS:UNIT], preferred_element_type=F32
        ).astype(BF16)
        for t in range(4):
            slots[j, 256:ROWS, t * 128 : (t + 1) * 128] = flat[t * 64 : (t + 1) * 64]
        rows = slots[j, :, 0:COLS]
        gate_acc[...] += lax.dot_general(rows, wg[:, cols(j)], NT, preferred_element_type=F32)
        up_acc[...] += lax.dot_general(rows, wu[:, cols(j)], NT, preferred_element_type=F32)

    def run(stages, count):
        last = max(lag for _, lag in stages)

        def tick(t, carry):
            for function, lag in stages:

                @pl.when((t >= lag) & (t < lag + count))
                def _(function=function, lag=lag):
                    function(t - lag)

            return carry

        lax.fori_loop(0, count + last, tick, 0)

    stats_send()
    ag_second(1)
    ag_start(3)
    ag_start(4)
    ag_second(2)
    ag_start(5)
    ag_start(6)
    ag_start(7)
    ag_second(3)
    ag_third(1)
    ag_second(4)
    ag_third(2)
    ag_second(5)
    ag_second(6)
    ag_second(7)
    scale_start()
    columns_send()

    loads[3].wait()
    loads[4].wait()
    wait(wg.at[FF : 2 * FF], wr.at[0])
    wait(wu.at[FF : 2 * FF], wr.at[1])
    def ag_tick(n, carry):
        @pl.when((n > 0) & (n + 2 < AG_RELAYED))
        def _():
            ag_third(n + 2)

        ag_use(n)

        @pl.when(n == 2)
        def _():
            scale_second()

        return carry

    lax.fori_loop(0, NZ, ag_tick, 0)
    wait(scales.at[scale_bundle(bm), :], scr.at[3])
    wait(scales.at[scale_bundle(bp), :], scr.at[4])
    wait(scales.at[scale_bundle(b2), :], scr.at[5])

    row = iota((ROWS, HEAD), 0)
    col = iota((ROWS, HEAD), 1)
    over = row - 256
    block_of = jnp.where(row < 256, lax.div(row, MAIN), lax.div(over, REM))
    slot_of = jnp.where(row < 256, lax.rem(row, MAIN), MAIN + lax.rem(over + 256, REM))
    pick = jnp.where(col == block_of * 8, 1.0, 0.0)
    spread = jnp.dot(pick, scales[...], precision=HIGH, preferred_element_type=F32)
    factor = jnp.sum(jnp.where(col == slot_of, spread, 0.0), axis=1, keepdims=True)
    gated = gate_acc[...] * factor
    hid[...] = (gated / (1.0 + jnp.exp(-gated)) * (up_acc[...] * factor)).astype(BF16)
    loads[5].wait()
    wait(wd.at[FF : 2 * FF], wr.at[2])

    def rs_chunk(n):
        odd = lax.rem(n, 2)
        return chunk(odd * (4 - lax.div(n + 1, 2)) - (1 - odd) * (4 - lax.div(n, 2)))

    def rs_start(n):
        j = rs_chunk(n)
        out = jnp.dot(hid[...], wd[:, cols(j)], preferred_element_type=F32).astype(BF16)
        part[n, :, 0:COLS] = out[0:256]
        rest = jnp.concatenate([out[256:, t * 128 : (t + 1) * 128] for t in range(4)], axis=0)
        part[n, :, COLS:UNIT] = jnp.dot(unperm[...], rest, preferred_element_type=F32).astype(BF16)

        @pl.when(n < RS_RELAYED)
        def _():
            remote(
                part.at[n, first_half(b2), :], r1p.at[n], rss.at[0, n], rsr.at[0, n], to_bp
            ).start()
            remote(
                part.at[n, second_half(b2), :], r1m.at[n], rss.at[1, n], rsr.at[1, n], to_bm
            ).start()

        @pl.when(n >= RS_RELAYED)
        def _():
            remote(part.at[n, bundle(b2), :], r2x.at[n], rss.at[0, n], rsr.at[0, n], to_b2).start()
            remote(part.at[n, bundle(bp), :], r2p.at[n], rss.at[2, n], rsr.at[2, n], to_bp).start()
            remote(part.at[n, bundle(bm), :], r2m.at[n], rss.at[3, n], rsr.at[3, n], to_bm).start()

        @pl.when(n > 0)
        def _():
            wait(att.at[ag_chunk(n)], atr.at[n])

        out_copy(ag_chunk(n)).start()

        @pl.when(n == 7)
        def _():
            logits = token_stats()[0]
            one = jnp.sum(jnp.where(number == first_id, logits, 0.0), axis=0, keepdims=True)
            two = jnp.sum(jnp.where(number == second_id, logits, 0.0), axis=0, keepdims=True)
            gate = 1.0 / (1.0 + jnp.exp(two - one))
            gates = jnp.where(first_id == number, gate, 1.0 - gate)
            spread = jnp.concatenate(
                [jnp.broadcast_to(gates[k : k + 1, :], (2 * MAIN, TOK)) for k in range(NZ)], axis=0
            )
            spread = spread * place[...].astype(F32)
            turned = lax.dot_general(eye, spread, NT, precision=HIGH, preferred_element_type=F32)
            high = turned.astype(BF16)
            wgt_hi[...] = high
            wgt_lo[...] = (turned - high.astype(F32)).astype(BF16)

    def add(n, rows, lanes, more):
        value = part[n, rows, lanes].astype(F32)
        for term in more:
            value = value + term.astype(F32)
        return value

    every = slice(0, UNIT)

    def rs_first(n):
        @pl.when(n < RS_RELAYED)
        def _():
            wait(r1p.at[n], rsr.at[0, n])
            rows = first_half(bp)
            part[n, rows, every] = add(n, rows, every, [r1p[n]]).astype(BF16)
            remote(part.at[n, bundle(bp), :], r2p.at[n], rss.at[2, n], rsr.at[2, n], to_bp).start()
            wait(r1m.at[n], rsr.at[1, n])
            rows = second_half(bm)
            part[n, rows, every] = add(n, rows, every, [r1m[n]]).astype(BF16)
            remote(part.at[n, bundle(bm), :], r2m.at[n], rss.at[3, n], rsr.at[3, n], to_bm).start()

    def rs_second(n):
        wait(r2p.at[n], rsr.at[2, n])
        wait(r2m.at[n], rsr.at[3, n])
        rows = bundle(b)

        @pl.when(n < RS_RELAYED)
        def _():
            part[n, rows, every] = add(n, rows, every, [r2p[n], r2m[n]]).astype(BF16)

        @pl.when(n >= RS_RELAYED)
        def _():
            wait(r2x.at[n], rsr.at[0, n])
            part[n, rows, every] = add(n, rows, every, [r2p[n], r2m[n], r2x[n]]).astype(BF16)

        remote(part.at[n, unit(a2, b), :], r4x.at[n], rss.at[4, n], rsr.at[4, n], to_a2).start()
        remote(part.at[n, unit(ap, b), :], r4p.at[n], rss.at[5, n], rsr.at[5, n], to_ap).start()
        remote(part.at[n, unit(am, b), :], r4m.at[n], rss.at[6, n], rsr.at[6, n], to_am).start()

    def rs_last(n):
        wait(r4p.at[n], rsr.at[5, n])
        wait(r4m.at[n], rsr.at[6, n])
        wait(r4x.at[n], rsr.at[4, n])
        zout[n] = add(n, unit(a, b), every, [r4p[n], r4m[n], r4x[n]]).astype(BF16)

        @pl.when(n < 7)
        def _():
            remote(zout.at[n], fin.at[e], z2s.at[n], z2r.at[7 - n], (c, rs_chunk(n))).start()

        @pl.when(n == 7)
        def _():
            fin[e] = zout[7]

    run(((rs_start, 0),), NZ)
    run(((rs_last, 10), (rs_second, 6), (rs_first, 0)), NZ)

    for n in range(1, NZ):
        wait(fin.at[ag_chunk(n)], z2r.at[n])
    for k in range(NZ):
        at = k * 2 * MAIN
        terms[at : at + MAIN, :] = fin[k, :, 0:COLS]
        rest = fin[k, :, COLS:UNIT].astype(F32)
        for t in range(4):
            terms[at + MAIN : at + 2 * MAIN, t * 128 : (t + 1) * 128] = jnp.where(
                tile == t, rest, 0.0
            ).astype(BF16)
    mixed = jnp.dot(wgt_hi[...], terms[...], preferred_element_type=F32)
    mixed = mixed + jnp.dot(wgt_lo[...], terms[...], preferred_element_type=F32)
    mixed_out[...] = mixed.astype(BF16)
    mix_copy = pltpu.make_async_copy(mixed_out, mix_out, ld.at[11])
    mix_copy.start()

    for i in range(15):
        wait(mine_kv, kvs.at[i])
    for i in range(4):
        wait(kv.at[0 : 4 * TOK, :], kvs.at[15 + i])
    for i, ref in enumerate((wg, wu, wd)):
        wait(ref.at[FF : 2 * FF], ws.at[i])
    for i, lanes, sem, _ in moves:
        wait(zs.at[i, :, lanes], z1s.at[sem])

    for i in range(15):
        wait(slots.at[0, 0:MAIN, :], dis.at[i])

    def drain(n, carry):
        @pl.when(n > 0)
        def _():
            for i, rows in enumerate((MAIN, MAIN, MAIN, 64, 64)):
                wait(slots.at[0, 0:rows, :], ags.at[i, n])

        @pl.when((n > 0) & (n < AG_RELAYED))
        def _():
            wait(slots.at[0, 0:32, :], ags.at[5, n])
            wait(slots.at[0, 0:32, :], ags.at[6, n])

        @pl.when(n >= AG_RELAYED)
        def _():
            wait(slots.at[0, 0:64, :], ags.at[5, n])

        @pl.when(n < RS_RELAYED)
        def _():
            wait(r1p.at[0], rss.at[0, n])
            wait(r1p.at[0], rss.at[1, n])

        @pl.when(n >= RS_RELAYED)
        def _():
            wait(r2x.at[0], rss.at[0, n])

        for i, piece in ((2, r2p), (3, r2m), (4, r4x), (5, r4p), (6, r4m)):
            wait(piece.at[0], rss.at[i, n])

        @pl.when(n < 7)
        def _():
            wait(zout.at[0], z2s.at[n])
            wait(zunits.at[0], zas.at[n + 1])
            wait(stats.at[0], sts.at[n + 1])
            wait(att.at[0], ats.at[n + 1])

        out_copy(n).wait()
        return carry

    lax.fori_loop(0, NZ, drain, 0)
    for i in range(6):
        wait(scales.at[0:8, :] if i < 3 else scales.at[0:32, :], scs.at[i])
    mix_copy.wait()


def hand_on(att_in, mix_in, att_out, mix_out, att_near, mix_near, sem):
    parts = [(mix_in, mix_near, mix_out, slice(0, TOK))]
    parts += [(att_in, att_near, att_out, slice(at, at + MAIN)) for at in range(0, TOK, MAIN)]
    ins = [
        pltpu.make_async_copy(src.at[rows, :], near.at[rows, :], sem.at[0, i])
        for i, (src, near, _, rows) in enumerate(parts)
    ]
    outs = [
        pltpu.make_async_copy(near.at[rows, :], dst.at[rows, :], sem.at[1, i])
        for i, (_, near, dst, rows) in enumerate(parts)
    ]
    for copy in ins:
        copy.start()
    for copy, out in zip(ins, outs):
        copy.wait()
        out.start()
    for out in outs:
        out.wait()


def local(
    query, key_states, value_states, residual, out_weight, norm_gain, router_weight, expert_ids,
    gate_weight, up_weight, down_weight,
):
    anywhere = pl.BlockSpec(memory_space=pl.ANY)
    vmem = pltpu.VMEM
    dma = pltpu.SemaphoreType.DMA
    scratch = [
        vmem((1, D), F32),
        vmem((NZ, D), BF16),
        vmem((2, TOK), jnp.int32),
        vmem((TOK, COLS), BF16),
        vmem((TOK, GROUPS * HEAD), BF16),
        vmem((SEQ, 2 * HEAD), BF16),
        vmem((GROUPS * TOK, HEAD), BF16),
        vmem((GROUPS * TOK, HEAD), F32),
        vmem((GROUPS * TOK, HEAD), F32),
        vmem((GROUPS * TOK, HEAD), F32),
        vmem((TOK, GROUPS * HEAD), BF16),
        vmem((GROUPS * HEAD, D), BF16),
        vmem((TOK, COLS), BF16),
        vmem((2 * FF, D), BF16),
        vmem((2 * FF, D), BF16),
        vmem((2 * FF, D), BF16),
        vmem((7, TOK, COLS), BF16),
        vmem((7, TOK, COLS), BF16),
        vmem((NZ, TOK, COLS), BF16),
        vmem((NZ, 2 * NZ, 128), F32),
        vmem((NZ * 2 * MAIN, TOK), BF16),
        vmem((256, 256), BF16),
        vmem((256, 256), BF16),
        vmem((NZ, MAIN, UNIT), BF16),
        vmem((NZ, ROWS, UNIT), BF16),
        vmem((NB * 8, HEAD), F32),
        vmem((ROWS, 2 * FF), F32),
        vmem((ROWS, 2 * FF), F32),
        vmem((ROWS, 2 * FF), BF16),
        vmem((TOK, NZ * 2 * MAIN), BF16),
        vmem((TOK, NZ * 2 * MAIN), BF16),
        vmem((NZ, 256, UNIT), BF16),
        vmem((NZ, 32, UNIT), BF16),
        vmem((NZ, 32, UNIT), BF16),
        vmem((NZ, 64, UNIT), BF16),
        vmem((NZ, 64, UNIT), BF16),
        vmem((NZ, 64, UNIT), BF16),
        vmem((NZ, MAIN, UNIT), BF16),
        vmem((NZ, MAIN, UNIT), BF16),
        vmem((NZ, MAIN, UNIT), BF16),
        vmem((NZ, MAIN, UNIT), BF16),
        vmem((NZ, MAIN, UNIT), BF16),
        vmem((NZ * 2 * MAIN, COLS), BF16),
        dma((12,)),
        dma((19,)),
        dma((20,)),
        dma((3,)),
        dma((3,)),
        dma((8,)),
        dma((8,)),
        dma((8,)),
        dma((8,)),
        dma((15,)),
        dma((16,)),
        dma((8,)),
        dma((8,)),
        dma((8,)),
        dma((8,)),
        dma((7, NZ)),
        dma((7, NZ)),
        dma((6,)),
        dma((6,)),
        dma((7, NZ)),
        dma((7, NZ)),
        dma((8,)),
        dma((8,)),
        dma((NZ,)),
    ]
    results = pl.pallas_call(
        kernel,
        out_shape=(
            jax.ShapeDtypeStruct((TOK, D), BF16),
            jax.ShapeDtypeStruct((TOK, COLS), BF16),
        ),
        in_specs=[anywhere] * 11,
        out_specs=(anywhere, anywhere),
        scratch_shapes=scratch,
        compiler_params=pltpu.CompilerParams(
            collective_id=0, has_side_effects=True, vmem_limit_bytes=56 * 1024 * 1024
        ),
        name="layer",
    )(
        query,
        key_states,
        value_states,
        residual,
        out_weight,
        norm_gain.reshape(1, D),
        router_weight.T,
        expert_ids.T,
        jnp.swapaxes(gate_weight, 1, 2),
        jnp.swapaxes(up_weight, 1, 2),
        down_weight,
    )
    return pl.pallas_call(
        hand_on,
        out_shape=tuple(jax.ShapeDtypeStruct(r.shape, r.dtype) for r in results),
        in_specs=[anywhere] * 2,
        out_specs=(anywhere, anywhere),
        scratch_shapes=[vmem((TOK, D), BF16), vmem((TOK, COLS), BF16), dma((2, 5))],
        compiler_params=pltpu.CompilerParams(vmem_limit_bytes=60 * 1024 * 1024),
        name="hand_on",
    )(*results)


def solution(mesh):
    placed = (
        P("ctx", "exp"),
        P("ctx", "exp"),
        P("ctx", "exp"),
        P("ctx", None),
        P("exp", None),
        P(),
        P(),
        P("ctx", None),
        P("exp", None, "ctx"),
        P("exp", None, "ctx"),
        P("exp", "ctx", None),
    )
    return jax.shard_map(
        local,
        mesh=mesh,
        in_specs=placed,
        out_specs=(P("ctx", None), P("ctx", "exp")),
        check_vma=False,
    )
```

```python
import functools
import math

import jax
import jax.numpy as jnp
from jax import lax
from jax.experimental import pallas as pl
from jax.experimental.pallas import tpu as pltpu
from jax.sharding import PartitionSpec as P

WINDOW = 4096
SEQ = 2048
D = 4096
TOK = 64
CAP = 20
FF = 224
NZ = 8
COLS = D // NZ
HEAD = 128
GROUPS = 4
NB = 16
MAIN = 16
REM = CAP - MAIN
UNIT = COLS + 128
BUNDLE = 4 * TOK
ROWS = NB * CAP
F32 = jnp.float32
BF16 = jnp.bfloat16
MESH = pl.DeviceIdType.MESH
HIGH = lax.Precision.HIGHEST
NT = (((1,), (1,)), ((), ()))

RS_LAGS = (3, 6, 9)
AG_RELAYED = 7
RS_RELAYED = 8


def iota(shape, dim):
    return lax.broadcasted_iota(jnp.int32, shape, dim)


def remote(src, dst, send, recv, device):
    return pltpu.make_async_remote_copy(
        src_ref=src, dst_ref=dst, send_sem=send, recv_sem=recv, device_id=device, device_id_type=MESH
    )


def wait(ref, sem):
    pltpu.make_async_copy(ref, ref, sem).wait()


def kernel(
    q_ref, k_ref, v_ref, res_ref, wo_ref, gain_hbm, rt_hbm, ids_hbm, wg_ref, wu_ref, wd_ref,
    att_out, mix_out,
    gain_ref, rt_ref, ids_ref, mixed_out, qv, kv, qs, top, tot, acc, attn, wo, res, wg, wu, wd,
    zs, zr, att, stats, place, perm, unperm, zunits,
    slots, scales, gate_acc, up_acc, hid, wgt_hi, wgt_lo,
    part, r1p, r1m, r2p, r2m, r2x, r4p, r4m, r4x, zout, fin, terms,
    ld, kvs, kvr, ws, wr, z1s, z1r, zas, zar, dis, dir_, sts, str_, ats, atr, ags, agr, scs, scr, rss, rsr,
    z2s, z2r, outs,
):
    c = lax.axis_index("ctx")
    e = lax.axis_index("exp")
    core = lax.rem(c, 2)
    chip = lax.div(c, 2)
    x = lax.rem(chip, 4)
    y = lax.div(chip, 4)
    a = x + core * (y - x)
    b = y + core * (x - y)

    def ctx_of(aa, bb):
        return ((bb + core * (aa - bb)) * 4 + aa + core * (bb - aa)) * 2 + core

    ap, am, a2 = lax.rem(a + 1, 4), lax.rem(a + 3, 4), lax.rem(a + 2, 4)
    bp, bm, b2 = lax.rem(b + 1, 4), lax.rem(b + 3, 4), lax.rem(b + 2, 4)
    to_ap, to_am, to_a2 = (ctx_of(ap, b), e), (ctx_of(am, b), e), (ctx_of(a2, b), e)
    to_bp, to_bm, to_b2 = (ctx_of(a, bp), e), (ctx_of(a, bm), e), (ctx_of(a, b2), e)

    def chunk(s):
        return lax.rem(e + s + NZ, NZ)

    def to_z(s):
        return (c, chunk(s))

    to_sib = (c + 1 - 2 * core, e)

    loads = [
        pltpu.make_async_copy(q_ref, qv, ld.at[0]),
        pltpu.make_async_copy(wo_ref, wo, ld.at[1]),
        pltpu.make_async_copy(
            res_ref.at[:, pl.ds(pl.multiple_of(e * COLS, COLS), COLS)], res, ld.at[2]
        ),
        pltpu.make_async_copy(wg_ref.at[0], wg.at[0:FF], ld.at[3]),
        pltpu.make_async_copy(wu_ref.at[0], wu.at[0:FF], ld.at[4]),
        pltpu.make_async_copy(wd_ref.at[0], wd.at[0:FF], ld.at[5]),
        pltpu.make_async_copy(gain_hbm, gain_ref, ld.at[8]),
        pltpu.make_async_copy(rt_hbm, rt_ref, ld.at[9]),
    ]

    def kv_rows(kk, bb, aa, units=1):
        return pl.ds(pl.multiple_of((kk * NB + bb * 4 + aa) * TOK, TOK), units * TOK)

    own = kv_rows(core, b, a)
    own_k = pltpu.make_async_copy(k_ref, kv.at[own, 0:HEAD], ld.at[6])
    own_v = pltpu.make_async_copy(v_ref, kv.at[own, HEAD : 2 * HEAD], ld.at[7])

    steps = [(da, db) for db in (0, 1, 3, 2) for da in (0, 1, 3, 2) if da + db > 0]

    def at_step(da, db):
        return lax.rem(a + da, 4), lax.rem(b + db, 4)

    own_ids = pltpu.make_async_copy(ids_hbm, ids_ref, ld.at[10])
    own_k.start()
    own_v.start()
    barrier = pltpu.get_barrier_semaphore()
    for da, db in steps:
        pl.semaphore_signal(
            barrier, inc=1, device_id=(ctx_of(*at_step(da, db)), e), device_id_type=MESH
        )
    for s in range(1, NZ):
        pl.semaphore_signal(barrier, inc=1, device_id=to_z(s), device_id_type=MESH)
    pl.semaphore_signal(barrier, inc=1, device_id=to_sib, device_id_type=MESH)
    for s in (1, -1):
        for da in (1, 2, 3):
            other = (ctx_of(*at_step(da, 0)), chunk(s))
            pl.semaphore_signal(barrier, inc=1, device_id=other, device_id_type=MESH)
    loads[0].start()
    own_ids.start()
    own_k.wait()
    own_v.wait()
    pl.semaphore_wait(barrier, len(steps) + NZ + 6)

    mine_kv = kv.at[own, :]
    for i, (da, db) in enumerate(steps):
        device = (ctx_of(*at_step(da, db)), e)
        remote(mine_kv, mine_kv, kvs.at[i], kvr.at[db * 4 + da], device).start()
    for copy in loads[1:]:
        copy.start()

    own_ids.wait()
    ids = ids_ref[...]
    first_id, second_id = ids[0:1, :], ids[1:2, :]
    number = iota((NZ, TOK), 0)
    named = jnp.where((first_id == number) | (second_id == number), 1.0, 0.0)
    before = jnp.where(iota((TOK, TOK), 0) < iota((TOK, TOK), 1), 1.0, 0.0).astype(BF16)
    slot = jnp.dot(named.astype(BF16), before, preferred_element_type=F32)
    slot = jnp.where(named > 0.0, slot, -1.0)
    row = iota((2 * MAIN, TOK), 0)
    wanted = jnp.where(row < MAIN, row, MAIN + lax.rem(row, REM)).astype(F32)
    for k in range(NZ):
        here = jnp.broadcast_to(slot[k : k + 1, :], (2 * MAIN, TOK)) == wanted
        place[k * 2 * MAIN : (k + 1) * 2 * MAIN, :] = jnp.where(here, 1.0, 0.0).astype(BF16)
    my_slot = jnp.sum(jnp.where(number == e, slot, 0.0), axis=0, keepdims=True)
    by_token = jnp.where(
        jnp.broadcast_to(my_slot, (HEAD, TOK)) == iota((HEAD, TOK), 0).astype(F32), 1.0, 0.0
    ).astype(BF16)
    eye = jnp.where(iota((TOK, TOK), 0) == iota((TOK, TOK), 1), 1.0, 0.0)
    slot_of_token = lax.dot_general(eye.astype(BF16), by_token, NT, preferred_element_type=F32)

    r256, l256 = iota((256, 256), 0), iota((256, 256), 1)
    i64 = lax.rem(r256, 64)
    to_unit = lax.div(i64, REM) * 16 + lax.div(r256, 64) * REM + lax.rem(i64, REM)
    perm[...] = jnp.where(l256 == to_unit, 1.0, 0.0).astype(BF16)
    to_flat = lax.rem(lax.div(r256, REM), 4) * 64 + lax.div(r256, 16) * REM + lax.rem(r256, REM)
    unperm[...] = jnp.where(l256 == to_flat, 1.0, 0.0).astype(BF16)

    gate_acc[...] = jnp.zeros_like(gate_acc)
    up_acc[...] = jnp.zeros_like(up_acc)
    half = COLS // 2
    stats[e] = jnp.zeros((2 * NZ, 128), F32)
    top[...] = jnp.full(top.shape, -1e30, F32)
    tot[...] = jnp.zeros_like(tot)
    acc[...] = jnp.zeros_like(acc)

    loads[0].wait()
    for g in range(GROUPS):
        qs[g * TOK : (g + 1) * TOK, :] = qv[:, g * HEAD : (g + 1) * HEAD]

    klane, vlane = slice(0, HEAD), slice(HEAD, 2 * HEAD)

    def row_wait(db, bb):
        for da in range(4):
            if da + db > 0:
                wait(kv.at[kv_rows(core, bb, lax.rem(a + 4 - da, 4)), :], kvr.at[db * 4 + da])

    def row_pass(i, bb):
        rows = kv.at[kv_rows(core, bb, 0, 4), :]
        remote(rows, rows, kvs.at[15 + i], kvr.at[16 + i], to_sib).start()

    query_pos = c * TOK + lax.rem(iota((GROUPS * TOK, 1), 0), TOK)
    lane = iota((1, BUNDLE), 1)
    score_scale = 1.0 / math.sqrt(HEAD)

    def attend(kk, bb):
        rows = kv_rows(kk, bb, 0, 4)
        key_pos = (
            TOK * kk
            + lax.rem(lane, TOK)
            + 2 * TOK * ((1 + 3 * kk) * lax.div(lane, TOK) + (4 - 3 * kk) * bb)
        )
        scores = (
            lax.dot_general(qs[...], kv[rows, klane], NT, preferred_element_type=F32) * score_scale
        )
        allowed = key_pos <= query_pos
        if SEQ > WINDOW:
            allowed = allowed & (key_pos > query_pos - WINDOW)
        scores = jnp.where(allowed, scores, -1e30)
        old = top[:, 0:1]
        new = jnp.maximum(old, jnp.max(scores, axis=1, keepdims=True))
        fade = jnp.exp(old - new)
        weights = jnp.exp(scores - new)
        top[...] = jnp.broadcast_to(new, top.shape)
        tot[...] = tot[...] * fade + jnp.sum(weights, axis=1, keepdims=True)
        acc[...] = acc[...] * fade + jnp.dot(
            weights.astype(BF16), kv[rows, vlane], preferred_element_type=F32
        )

    def other_wait(i, aa):
        wait(kv.at[kv_rows(1 - core, aa, 0, 4), :], kvr.at[16 + i])

    row_wait(0, b)
    row_pass(0, b)
    attend(core, b)
    other_wait(0, a)
    attend(1 - core, a)
    row_wait(1, bm)
    row_pass(1, bm)
    row_wait(3, bp)
    row_pass(2, bp)
    attend(core, bm)
    attend(core, bp)
    row_wait(2, b2)
    row_pass(3, b2)
    for i, (src, dst) in enumerate(((wg_ref, wg), (wu_ref, wu), (wd_ref, wd))):
        remote(src.at[0], dst.at[FF : 2 * FF], ws.at[i], wr.at[i], to_sib).start()
    other_wait(1, am)
    attend(1 - core, am)
    other_wait(2, ap)
    attend(1 - core, ap)
    attend(core, b2)
    other_wait(3, a2)
    attend(1 - core, a2)

    for g in range(GROUPS):
        rows = slice(g * TOK, (g + 1) * TOK)
        attn[:, g * HEAD : (g + 1) * HEAD] = (acc[rows, :] / tot[rows, 0:1]).astype(BF16)

    def cols(j):
        return pl.ds(pl.multiple_of(j * COLS, COLS), COLS)

    def project(s):
        return jnp.dot(attn[...], wo[:, cols(chunk(s))], preferred_element_type=F32)

    lo, hi = slice(0, half), slice(half, COLS)
    full = slice(0, COLS)
    moves = (
        (0, lo, 0, 2), (0, hi, 7, -2), (1, full, 1, 1), (2, full, 2, -1), (3, full, 3, 1), (4, full, 4, -1),
        (5, full, 5, 2), (6, full, 6, -2),
    )

    def sum_send(k):
        i, lanes, sem, step = moves[k]
        remote(
            zs.at[i, :, lanes], zr.at[i, :, lanes], z1s.at[sem], z1r.at[sem], to_z(step)
        ).start()

    def sum_wait(k):
        i, lanes, sem, _ = moves[k]
        wait(zr.at[i, :, lanes], z1r.at[sem])

    loads[1].wait()
    zs[0] = project(4).astype(BF16)
    sum_send(0)
    sum_send(1)
    for i, s in ((1, 3), (2, -3), (3, 1), (4, -1)):
        zs[i] = project(s).astype(BF16)
        sum_send(i + 1)
    up, down = project(2), project(-2)
    loads[2].wait()
    total = project(0) + res[...].astype(F32)
    sum_wait(2)
    sum_wait(0)
    up = up + zr[1].astype(F32)
    zs[5, :, lo] = (up[:, lo] + zr[0, :, lo].astype(F32)).astype(BF16)
    zs[5, :, hi] = up[:, hi].astype(BF16)
    sum_send(6)
    sum_wait(3)
    sum_wait(1)
    down = down + zr[2].astype(F32)
    zs[6, :, hi] = (down[:, hi] + zr[0, :, hi].astype(F32)).astype(BF16)
    zs[6, :, lo] = down[:, lo].astype(BF16)
    sum_send(7)
    sum_wait(4)
    sum_wait(5)
    total = total + zr[3].astype(F32) + zr[4].astype(F32)
    sum_wait(6)
    sum_wait(7)
    total = (total + zr[5].astype(F32) + zr[6].astype(F32)).astype(BF16)
    att[e] = total

    loads[6].wait()
    loads[7].wait()
    def unit(aa, bb):
        return pl.ds(pl.multiple_of((bb * 4 + aa) * MAIN, MAIN), MAIN)

    tile = lax.div(iota((MAIN, 128), 0), REM)
    value = total.astype(F32)
    scaled = (value * gain_ref[:, cols(e)]).astype(BF16)
    packed = jnp.dot(place[...], scaled, preferred_element_type=F32)
    for k in range(NZ):
        at = k * 2 * MAIN
        zunits[k, :, 0:COLS] = packed[at : at + MAIN].astype(BF16)
        rest = jnp.zeros((MAIN, 128), F32)
        for t in range(4):
            rest = rest + jnp.where(
                tile == t, packed[at + MAIN : at + 2 * MAIN, t * 128 : (t + 1) * 128], 0.0
            )
        zunits[k, :, COLS:UNIT] = rest.astype(BF16)
    spread_steps = ((1, 2), (-1, 1), (2, 4), (-2, 3), (3, 6), (-3, 5), (4, 7))
    first_steps = ((1, 0), (3, 1), (2, 2))
    mine_rows = unit(a, b)
    for s, n in spread_steps:
        src, dst = zunits.at[chunk(s)], slots.at[e, mine_rows, :]
        remote(src, dst, zas.at[n], zar.at[n], to_z(s)).start()
        if n < 3:
            for da, i in first_steps:
                device = (ctx_of(*at_step(da, 0)), chunk(s))
                remote(src, dst, ags.at[i, n], agr.at[i, n], device).start()
    slots[e, mine_rows, :] = zunits[e]
    here = slots.at[e, mine_rows, :]
    for da, i in first_steps:
        remote(here, here, ags.at[i, 0], agr.at[i, 0], (ctx_of(*at_step(da, 0)), e)).start()
    squares = jnp.sum(value * value, axis=1, keepdims=True)
    stats[e, 0:NZ, 0:TOK] = lax.dot_general(
        rt_ref[:, cols(e)], scaled, NT, preferred_element_type=F32
    )
    stats[e, NZ : 2 * NZ, 0:TOK] = jnp.broadcast_to(
        jnp.sum(eye * squares, axis=0, keepdims=True), (NZ, TOK)
    )

    def ag_chunk(n):
        odd = lax.rem(n, 2)
        return chunk((2 * odd - 1) * lax.div(n + 1, 2))

    def bundle(bb):
        return pl.ds(pl.multiple_of(bb * 64, 64), 64)

    def first_half(bb):
        return pl.ds(pl.multiple_of(bb * 64, 32), 32)

    def second_half(bb):
        return pl.ds(pl.multiple_of(bb * 64 + 32, 32), 32)

    def scale_unit(aa, bb):
        return pl.ds(pl.multiple_of((bb * 4 + aa) * 8, 8), 8)

    def scale_bundle(bb):
        return pl.ds(pl.multiple_of(bb * 32, 8), 32)

    def out_copy(j):
        return pltpu.make_async_copy(att.at[j], att_out.at[:, cols(j)], outs.at[j])

    def token_stats():
        whole = stats[0]
        for k in range(1, NZ):
            whole = whole + stats[k]
        inverse = lax.rsqrt(whole[NZ : NZ + 1, 0:TOK] * (1.0 / D) + 1e-05)
        return whole[0:NZ, 0:TOK] * inverse, inverse

    def stats_send():
        for s, k in spread_steps:
            remote(stats.at[e], stats.at[e], sts.at[k], str_.at[k], to_z(s)).start()

    def columns_send():
        for s, k in spread_steps:
            remote(att.at[e], att.at[e], ats.at[k], atr.at[k], to_z(s)).start()

    def ag_start(n):
        here = slots.at[ag_chunk(n), mine_rows, :]
        wait(here, zar.at[n])
        remote(here, here, ags.at[0, n], agr.at[0, n], to_ap).start()
        remote(here, here, ags.at[1, n], agr.at[1, n], to_am).start()
        remote(here, here, ags.at[2, n], agr.at[2, n], to_a2).start()

    def scale_start():
        for k in range(1, NZ):
            wait(stats.at[ag_chunk(k)], str_.at[k])
        inverse = token_stats()[1]
        inverse = jnp.sum(eye * inverse, axis=1, keepdims=True)
        by_slot = jnp.sum(slot_of_token * inverse, axis=0, keepdims=True)
        scales[scale_unit(a, b), :] = jnp.broadcast_to(by_slot, (8, HEAD))
        here = scales.at[scale_unit(a, b), :]
        remote(here, here, scs.at[0], scr.at[0], to_ap).start()
        remote(here, here, scs.at[1], scr.at[1], to_am).start()
        remote(here, here, scs.at[2], scr.at[2], to_a2).start()

    def scale_second():
        wait(scales.at[scale_unit(am, b), :], scr.at[0])
        wait(scales.at[scale_unit(ap, b), :], scr.at[1])
        wait(scales.at[scale_unit(a2, b), :], scr.at[2])
        piece = scales.at[scale_bundle(b), :]
        remote(piece, piece, scs.at[3], scr.at[3], to_bp).start()
        remote(piece, piece, scs.at[4], scr.at[4], to_bm).start()
        remote(piece, piece, scs.at[5], scr.at[5], to_b2).start()

    def ag_second(n):
        j = ag_chunk(n)
        if isinstance(n, int) and 0 < n < 3:
            wait(slots.at[j, mine_rows, :], zar.at[n])
        wait(slots.at[j, unit(am, b), :], agr.at[0, n])
        wait(slots.at[j, unit(ap, b), :], agr.at[1, n])
        wait(slots.at[j, unit(a2, b), :], agr.at[2, n])
        piece = slots.at[j, bundle(b), :]
        remote(piece, piece, ags.at[3, n], agr.at[3, n], to_bp).start()
        remote(piece, piece, ags.at[4, n], agr.at[4, n], to_bm).start()

        @pl.when(n >= AG_RELAYED)
        def _():
            remote(piece, piece, ags.at[5, n], agr.at[5, n], to_b2).start()

    def ag_third(n):
        j = ag_chunk(n)

        wait(slots.at[j, bundle(bm), :], agr.at[3, n])
        piece = slots.at[j, first_half(bm), :]
        remote(piece, piece, ags.at[5, n], agr.at[5, n], to_bp).start()
        wait(slots.at[j, bundle(bp), :], agr.at[4, n])
        piece = slots.at[j, second_half(bp), :]
        remote(piece, piece, ags.at[6, n], agr.at[6, n], to_bm).start()

    def ag_use(n):
        j = ag_chunk(n)

        @pl.when(n < AG_RELAYED)
        def _():
            wait(slots.at[j, first_half(b2), :], agr.at[5, n])
            wait(slots.at[j, second_half(b2), :], agr.at[6, n])

        @pl.when(n >= AG_RELAYED)
        def _():
            wait(slots.at[j, bundle(bm), :], agr.at[3, n])
            wait(slots.at[j, bundle(bp), :], agr.at[4, n])
            wait(slots.at[j, bundle(b2), :], agr.at[5, n])

        flat = jnp.dot(
            perm[...], slots[j, 0:256, COLS:UNIT], preferred_element_type=F32
        ).astype(BF16)
        for t in range(4):
            slots[j, 256:ROWS, t * 128 : (t + 1) * 128] = flat[t * 64 : (t + 1) * 64]
        rows = slots[j, :, 0:COLS]
        gate_acc[...] += lax.dot_general(rows, wg[:, cols(j)], NT, preferred_element_type=F32)
        up_acc[...] += lax.dot_general(rows, wu[:, cols(j)], NT, preferred_element_type=F32)

    def run(stages, count):
        last = max(lag for _, lag in stages)

        def tick(t, carry):
            for function, lag in stages:

                @pl.when((t >= lag) & (t < lag + count))
                def _(function=function, lag=lag):
                    function(t - lag)

            return carry

        lax.fori_loop(0, count + last, tick, 0)

    stats_send()
    ag_second(0)
    ag_second(1)
    ag_start(3)
    ag_start(4)
    ag_second(2)
    ag_start(5)
    ag_start(6)
    ag_start(7)
    ag_third(0)
    ag_second(3)
    ag_third(1)
    ag_second(4)
    ag_second(5)
    ag_third(2)
    ag_second(6)
    ag_third(3)
    ag_second(7)
    ag_third(4)
    scale_start()
    columns_send()

    loads[3].wait()
    loads[4].wait()
    wait(wg.at[FF : 2 * FF], wr.at[0])
    wait(wu.at[FF : 2 * FF], wr.at[1])
    def ag_tick(n, carry):
        @pl.when(n + 5 < AG_RELAYED)
        def _():
            ag_third(n + 5)

        ag_use(n)

        @pl.when(n == 2)
        def _():
            scale_second()

        return carry

    lax.fori_loop(0, NZ, ag_tick, 0)
    wait(scales.at[scale_bundle(bm), :], scr.at[3])
    wait(scales.at[scale_bundle(bp), :], scr.at[4])
    wait(scales.at[scale_bundle(b2), :], scr.at[5])

    row = iota((ROWS, HEAD), 0)
    col = iota((ROWS, HEAD), 1)
    over = row - 256
    block_of = jnp.where(row < 256, lax.div(row, MAIN), lax.div(over, REM))
    slot_of = jnp.where(row < 256, lax.rem(row, MAIN), MAIN + lax.rem(over + 256, REM))
    pick = jnp.where(col == block_of * 8, 1.0, 0.0)
    spread = jnp.dot(pick, scales[...], precision=HIGH, preferred_element_type=F32)
    factor = jnp.sum(jnp.where(col == slot_of, spread, 0.0), axis=1, keepdims=True)
    gated = gate_acc[...] * factor
    hid[...] = (gated / (1.0 + jnp.exp(-gated)) * (up_acc[...] * factor)).astype(BF16)
    loads[5].wait()
    wait(wd.at[FF : 2 * FF], wr.at[2])

    def rs_chunk(n):
        odd = lax.rem(n, 2)
        return chunk(odd * (4 - lax.div(n + 1, 2)) - (1 - odd) * (4 - lax.div(n, 2)))

    def rs_start(n):
        j = rs_chunk(n)
        out = jnp.dot(hid[...], wd[:, cols(j)], preferred_element_type=F32).astype(BF16)
        part[n, :, 0:COLS] = out[0:256]
        rest = jnp.concatenate([out[256:, t * 128 : (t + 1) * 128] for t in range(4)], axis=0)
        part[n, :, COLS:UNIT] = jnp.dot(unperm[...], rest, preferred_element_type=F32).astype(BF16)

        @pl.when(n < RS_RELAYED)
        def _():
            remote(
                part.at[n, first_half(b2), :], r1p.at[n], rss.at[0, n], rsr.at[0, n], to_bp
            ).start()
            remote(
                part.at[n, second_half(b2), :], r1m.at[n], rss.at[1, n], rsr.at[1, n], to_bm
            ).start()

        @pl.when(n >= RS_RELAYED)
        def _():
            remote(part.at[n, bundle(b2), :], r2x.at[n], rss.at[0, n], rsr.at[0, n], to_b2).start()
            remote(part.at[n, bundle(bp), :], r2p.at[n], rss.at[2, n], rsr.at[2, n], to_bp).start()
            remote(part.at[n, bundle(bm), :], r2m.at[n], rss.at[3, n], rsr.at[3, n], to_bm).start()

        @pl.when(n == 7)
        def _():
            logits = token_stats()[0]
            one = jnp.sum(jnp.where(number == first_id, logits, 0.0), axis=0, keepdims=True)
            two = jnp.sum(jnp.where(number == second_id, logits, 0.0), axis=0, keepdims=True)
            gate = 1.0 / (1.0 + jnp.exp(two - one))
            gates = jnp.where(first_id == number, gate, 1.0 - gate)
            spread = jnp.concatenate(
                [jnp.broadcast_to(gates[k : k + 1, :], (2 * MAIN, TOK)) for k in range(NZ)], axis=0
            )
            spread = spread * place[...].astype(F32)
            turned = lax.dot_general(eye, spread, NT, precision=HIGH, preferred_element_type=F32)
            high = turned.astype(BF16)
            wgt_hi[...] = high
            wgt_lo[...] = (turned - high.astype(F32)).astype(BF16)

    def add(n, rows, lanes, more):
        value = part[n, rows, lanes].astype(F32)
        for term in more:
            value = value + term.astype(F32)
        return value

    every = slice(0, UNIT)

    def rs_first(n):
        @pl.when(n < RS_RELAYED)
        def _():
            wait(r1p.at[n], rsr.at[0, n])
            rows = first_half(bp)
            part[n, rows, every] = add(n, rows, every, [r1p[n]]).astype(BF16)
            remote(part.at[n, bundle(bp), :], r2p.at[n], rss.at[2, n], rsr.at[2, n], to_bp).start()
            wait(r1m.at[n], rsr.at[1, n])
            rows = second_half(bm)
            part[n, rows, every] = add(n, rows, every, [r1m[n]]).astype(BF16)
            remote(part.at[n, bundle(bm), :], r2m.at[n], rss.at[3, n], rsr.at[3, n], to_bm).start()

    def rs_second(n):
        @pl.when(n > 0)
        def _():
            wait(att.at[ag_chunk(n)], atr.at[n])

        out_copy(ag_chunk(n)).start()
        wait(r2p.at[n], rsr.at[2, n])
        wait(r2m.at[n], rsr.at[3, n])
        rows = bundle(b)

        @pl.when(n < RS_RELAYED)
        def _():
            part[n, rows, every] = add(n, rows, every, [r2p[n], r2m[n]]).astype(BF16)

        @pl.when(n >= RS_RELAYED)
        def _():
            wait(r2x.at[n], rsr.at[0, n])
            part[n, rows, every] = add(n, rows, every, [r2p[n], r2m[n], r2x[n]]).astype(BF16)

        remote(part.at[n, unit(a2, b), :], r4x.at[n], rss.at[4, n], rsr.at[4, n], to_a2).start()
        remote(part.at[n, unit(ap, b), :], r4p.at[n], rss.at[5, n], rsr.at[5, n], to_ap).start()
        remote(part.at[n, unit(am, b), :], r4m.at[n], rss.at[6, n], rsr.at[6, n], to_am).start()

    def rs_last(n):
        wait(r4p.at[n], rsr.at[5, n])
        wait(r4m.at[n], rsr.at[6, n])
        wait(r4x.at[n], rsr.at[4, n])
        zout[n] = add(n, unit(a, b), every, [r4p[n], r4m[n], r4x[n]]).astype(BF16)

        @pl.when(n < 7)
        def _():
            remote(zout.at[n], fin.at[e], z2s.at[n], z2r.at[7 - n], (c, rs_chunk(n))).start()

        @pl.when(n == 7)
        def _():
            fin[e] = zout[7]

    run(((rs_start, 0),), NZ)
    run(((rs_last, 12), (rs_second, 7), (rs_first, 0)), NZ)

    for n in range(1, NZ):
        wait(fin.at[ag_chunk(n)], z2r.at[n])
    for k in range(NZ):
        at = k * 2 * MAIN
        terms[at : at + MAIN, :] = fin[k, :, 0:COLS]
        rest = fin[k, :, COLS:UNIT].astype(F32)
        for t in range(4):
            terms[at + MAIN : at + 2 * MAIN, t * 128 : (t + 1) * 128] = jnp.where(
                tile == t, rest, 0.0
            ).astype(BF16)
    mixed = jnp.dot(wgt_hi[...], terms[...], preferred_element_type=F32)
    mixed = mixed + jnp.dot(wgt_lo[...], terms[...], preferred_element_type=F32)
    mixed_out[...] = mixed.astype(BF16)
    mix_copy = pltpu.make_async_copy(mixed_out, mix_out, ld.at[11])
    mix_copy.start()

    for i in range(15):
        wait(mine_kv, kvs.at[i])
    for i in range(4):
        wait(kv.at[0 : 4 * TOK, :], kvs.at[15 + i])
    for i, ref in enumerate((wg, wu, wd)):
        wait(ref.at[FF : 2 * FF], ws.at[i])
    for i, lanes, sem, _ in moves:
        wait(zs.at[i, :, lanes], z1s.at[sem])


    def drain(n, carry):
        for i, rows in enumerate((MAIN, MAIN, MAIN, 64, 64)):
            wait(slots.at[0, 0:rows, :], ags.at[i, n])

        @pl.when(n < AG_RELAYED)
        def _():
            wait(slots.at[0, 0:32, :], ags.at[5, n])
            wait(slots.at[0, 0:32, :], ags.at[6, n])

        @pl.when(n >= AG_RELAYED)
        def _():
            wait(slots.at[0, 0:64, :], ags.at[5, n])

        @pl.when(n < RS_RELAYED)
        def _():
            wait(r1p.at[0], rss.at[0, n])
            wait(r1p.at[0], rss.at[1, n])

        @pl.when(n >= RS_RELAYED)
        def _():
            wait(r2x.at[0], rss.at[0, n])

        for i, piece in ((2, r2p), (3, r2m), (4, r4x), (5, r4p), (6, r4m)):
            wait(piece.at[0], rss.at[i, n])

        @pl.when(n < 7)
        def _():
            wait(zout.at[0], z2s.at[n])
            wait(zunits.at[0], zas.at[n + 1])
            wait(stats.at[0], sts.at[n + 1])
            wait(att.at[0], ats.at[n + 1])

        out_copy(n).wait()
        return carry

    lax.fori_loop(0, NZ, drain, 0)
    for i in range(6):
        wait(scales.at[0:8, :] if i < 3 else scales.at[0:32, :], scs.at[i])
    mix_copy.wait()


def hand_on(att_in, mix_in, att_out, mix_out, att_near, mix_near, sem):
    parts = [(mix_in, mix_near, mix_out, slice(0, TOK))]
    parts += [(att_in, att_near, att_out, slice(at, at + 32)) for at in range(0, TOK, 32)]
    ins = [
        pltpu.make_async_copy(src.at[rows, :], near.at[rows, :], sem.at[0, i])
        for i, (src, near, _, rows) in enumerate(parts)
    ]
    outs = [
        pltpu.make_async_copy(near.at[rows, :], dst.at[rows, :], sem.at[1, i])
        for i, (_, near, dst, rows) in enumerate(parts)
    ]
    for copy in ins:
        copy.start()
    for copy, out in zip(ins, outs):
        copy.wait()
        out.start()
    for out in outs:
        out.wait()


def local(
    query, key_states, value_states, residual, out_weight, norm_gain, router_weight, expert_ids,
    gate_weight, up_weight, down_weight,
):
    anywhere = pl.BlockSpec(memory_space=pl.ANY)
    vmem = pltpu.VMEM
    dma = pltpu.SemaphoreType.DMA
    scratch = [
        vmem((1, D), F32),
        vmem((NZ, D), BF16),
        vmem((2, TOK), jnp.int32),
        vmem((TOK, COLS), BF16),
        vmem((TOK, GROUPS * HEAD), BF16),
        vmem((SEQ, 2 * HEAD), BF16),
        vmem((GROUPS * TOK, HEAD), BF16),
        vmem((GROUPS * TOK, HEAD), F32),
        vmem((GROUPS * TOK, HEAD), F32),
        vmem((GROUPS * TOK, HEAD), F32),
        vmem((TOK, GROUPS * HEAD), BF16),
        vmem((GROUPS * HEAD, D), BF16),
        vmem((TOK, COLS), BF16),
        vmem((2 * FF, D), BF16),
        vmem((2 * FF, D), BF16),
        vmem((2 * FF, D), BF16),
        vmem((7, TOK, COLS), BF16),
        vmem((7, TOK, COLS), BF16),
        vmem((NZ, TOK, COLS), BF16),
        vmem((NZ, 2 * NZ, 128), F32),
        vmem((NZ * 2 * MAIN, TOK), BF16),
        vmem((256, 256), BF16),
        vmem((256, 256), BF16),
        vmem((NZ, MAIN, UNIT), BF16),
        vmem((NZ, ROWS, UNIT), BF16),
        vmem((NB * 8, HEAD), F32),
        vmem((ROWS, 2 * FF), F32),
        vmem((ROWS, 2 * FF), F32),
        vmem((ROWS, 2 * FF), BF16),
        vmem((TOK, NZ * 2 * MAIN), BF16),
        vmem((TOK, NZ * 2 * MAIN), BF16),
        vmem((NZ, 256, UNIT), BF16),
        vmem((NZ, 32, UNIT), BF16),
        vmem((NZ, 32, UNIT), BF16),
        vmem((NZ, 64, UNIT), BF16),
        vmem((NZ, 64, UNIT), BF16),
        vmem((NZ, 64, UNIT), BF16),
        vmem((NZ, MAIN, UNIT), BF16),
        vmem((NZ, MAIN, UNIT), BF16),
        vmem((NZ, MAIN, UNIT), BF16),
        vmem((NZ, MAIN, UNIT), BF16),
        vmem((NZ, MAIN, UNIT), BF16),
        vmem((NZ * 2 * MAIN, COLS), BF16),
        dma((12,)),
        dma((19,)),
        dma((20,)),
        dma((3,)),
        dma((3,)),
        dma((8,)),
        dma((8,)),
        dma((8,)),
        dma((8,)),
        dma((15,)),
        dma((16,)),
        dma((8,)),
        dma((8,)),
        dma((8,)),
        dma((8,)),
        dma((7, NZ)),
        dma((7, NZ)),
        dma((6,)),
        dma((6,)),
        dma((7, NZ)),
        dma((7, NZ)),
        dma((8,)),
        dma((8,)),
        dma((NZ,)),
    ]
    results = pl.pallas_call(
        kernel,
        out_shape=(
            jax.ShapeDtypeStruct((TOK, D), BF16),
            jax.ShapeDtypeStruct((TOK, COLS), BF16),
        ),
        in_specs=[anywhere] * 11,
        out_specs=(anywhere, anywhere),
        scratch_shapes=scratch,
        compiler_params=pltpu.CompilerParams(
            collective_id=0, has_side_effects=True, vmem_limit_bytes=56 * 1024 * 1024
        ),
        name="layer",
    )(
        query,
        key_states,
        value_states,
        residual,
        out_weight,
        norm_gain.reshape(1, D),
        router_weight.T,
        expert_ids.T,
        jnp.swapaxes(gate_weight, 1, 2),
        jnp.swapaxes(up_weight, 1, 2),
        down_weight,
    )
    return pl.pallas_call(
        hand_on,
        out_shape=tuple(jax.ShapeDtypeStruct(r.shape, r.dtype) for r in results),
        in_specs=[anywhere] * 2,
        out_specs=(anywhere, anywhere),
        scratch_shapes=[vmem((TOK, D), BF16), vmem((TOK, COLS), BF16), dma((2, 5))],
        compiler_params=pltpu.CompilerParams(vmem_limit_bytes=60 * 1024 * 1024),
        name="hand_on",
    )(*results)


def solution(mesh):
    placed = (
        P("ctx", "exp"),
        P("ctx", "exp"),
        P("ctx", "exp"),
        P("ctx", None),
        P("exp", None),
        P(),
        P(),
        P("ctx", None),
        P("exp", None, "ctx"),
        P("exp", None, "ctx"),
        P("exp", "ctx", None),
    )
    return jax.shard_map(
        local,
        mesh=mesh,
        in_specs=placed,
        out_specs=(P("ctx", None), P("ctx", "exp")),
        check_vma=False,
    )
```

```python
import functools
import math

import jax
import jax.numpy as jnp
from jax import lax
from jax.experimental import pallas as pl
from jax.experimental.pallas import tpu as pltpu
from jax.sharding import PartitionSpec as P

WINDOW = 4096
SEQ = 2048
D = 4096
TOK = 64
CAP = 20
FF = 224
NZ = 8
COLS = D // NZ
HEAD = 128
GROUPS = 4
NB = 16
MAIN = 16
REM = CAP - MAIN
UNIT = COLS + 128
BUNDLE = 4 * TOK
ROWS = NB * CAP
F32 = jnp.float32
BF16 = jnp.bfloat16
MESH = pl.DeviceIdType.MESH
HIGH = lax.Precision.HIGHEST
NT = (((1,), (1,)), ((), ()))

RS_LAGS = (3, 6, 9)
AG_RELAYED = 7
RS_RELAYED = 8


def iota(shape, dim):
    return lax.broadcasted_iota(jnp.int32, shape, dim)


def remote(src, dst, send, recv, device):
    return pltpu.make_async_remote_copy(
        src_ref=src, dst_ref=dst, send_sem=send, recv_sem=recv, device_id=device, device_id_type=MESH
    )


def wait(ref, sem):
    pltpu.make_async_copy(ref, ref, sem).wait()


def kernel(
    q_ref, k_ref, v_ref, res_ref, wo_ref, gain_hbm, rt_hbm, ids_hbm, wg_ref, wu_ref, wd_ref,
    att_out, mix_out,
    gain_ref, rt_ref, ids_ref, mixed_out, qv, kv, qs, top, tot, acc, attn, wo, res, wg, wu, wd,
    zs, zr, att, stats, place, perm, unperm, zunits,
    slots, scales, gate_acc, up_acc, hid, wgt_hi, wgt_lo,
    part, r1p, r1m, r2p, r2m, r2x, r4p, r4m, r4x, zout, fin, terms,
    ld, kvs, kvr, ws, wr, z1s, z1r, zas, zar, dis, dir_, sts, str_, ats, atr, ags, agr, scs, scr, rss, rsr,
    z2s, z2r, outs,
):
    c = lax.axis_index("ctx")
    e = lax.axis_index("exp")
    core = lax.rem(c, 2)
    chip = lax.div(c, 2)
    x = lax.rem(chip, 4)
    y = lax.div(chip, 4)
    a = x + core * (y - x)
    b = y + core * (x - y)

    def ctx_of(aa, bb):
        return ((bb + core * (aa - bb)) * 4 + aa + core * (bb - aa)) * 2 + core

    ap, am, a2 = lax.rem(a + 1, 4), lax.rem(a + 3, 4), lax.rem(a + 2, 4)
    bp, bm, b2 = lax.rem(b + 1, 4), lax.rem(b + 3, 4), lax.rem(b + 2, 4)
    to_ap, to_am, to_a2 = (ctx_of(ap, b), e), (ctx_of(am, b), e), (ctx_of(a2, b), e)
    to_bp, to_bm, to_b2 = (ctx_of(a, bp), e), (ctx_of(a, bm), e), (ctx_of(a, b2), e)

    def chunk(s):
        return lax.rem(e + s + NZ, NZ)

    def to_z(s):
        return (c, chunk(s))

    to_sib = (c + 1 - 2 * core, e)

    loads = [
        pltpu.make_async_copy(q_ref, qv, ld.at[0]),
        pltpu.make_async_copy(wo_ref, wo, ld.at[1]),
        pltpu.make_async_copy(
            res_ref.at[:, pl.ds(pl.multiple_of(e * COLS, COLS), COLS)], res, ld.at[2]
        ),
        pltpu.make_async_copy(wg_ref.at[0], wg.at[0:FF], ld.at[3]),
        pltpu.make_async_copy(wu_ref.at[0], wu.at[0:FF], ld.at[4]),
        pltpu.make_async_copy(wd_ref.at[0], wd.at[0:FF], ld.at[5]),
        pltpu.make_async_copy(gain_hbm, gain_ref, ld.at[8]),
        pltpu.make_async_copy(rt_hbm, rt_ref, ld.at[9]),
    ]

    def kv_rows(kk, bb, aa, units=1):
        return pl.ds(pl.multiple_of((kk * NB + bb * 4 + aa) * TOK, TOK), units * TOK)

    own = kv_rows(core, b, a)
    own_k = pltpu.make_async_copy(k_ref, kv.at[own, 0:HEAD], ld.at[6])
    own_v = pltpu.make_async_copy(v_ref, kv.at[own, HEAD : 2 * HEAD], ld.at[7])

    steps = [(da, db) for db in (0, 1, 3, 2) for da in (0, 1, 3, 2) if da + db > 0]

    def at_step(da, db):
        return lax.rem(a + da, 4), lax.rem(b + db, 4)

    own_ids = pltpu.make_async_copy(ids_hbm, ids_ref, ld.at[10])
    own_k.start()
    own_v.start()
    barrier = pltpu.get_barrier_semaphore()
    for da, db in steps:
        pl.semaphore_signal(
            barrier, inc=1, device_id=(ctx_of(*at_step(da, db)), e), device_id_type=MESH
        )
    for s in range(1, NZ):
        pl.semaphore_signal(barrier, inc=1, device_id=to_z(s), device_id_type=MESH)
    pl.semaphore_signal(barrier, inc=1, device_id=to_sib, device_id_type=MESH)
    for s in (1, -1):
        for da in (1, 2, 3):
            other = (ctx_of(*at_step(da, 0)), chunk(s))
            pl.semaphore_signal(barrier, inc=1, device_id=other, device_id_type=MESH)
    loads[0].start()
    own_ids.start()
    own_k.wait()
    own_v.wait()
    pl.semaphore_wait(barrier, len(steps) + NZ + 6)

    mine_kv = kv.at[own, :]
    for i, (da, db) in enumerate(steps):
        device = (ctx_of(*at_step(da, db)), e)
        remote(mine_kv, mine_kv, kvs.at[i], kvr.at[db * 4 + da], device).start()
    for copy in loads[1:]:
        copy.start()

    own_ids.wait()
    ids = ids_ref[...]
    first_id, second_id = ids[0:1, :], ids[1:2, :]
    number = iota((NZ, TOK), 0)
    named = jnp.where((first_id == number) | (second_id == number), 1.0, 0.0)
    before = jnp.where(iota((TOK, TOK), 0) < iota((TOK, TOK), 1), 1.0, 0.0).astype(BF16)
    slot = jnp.dot(named.astype(BF16), before, preferred_element_type=F32)
    slot = jnp.where(named > 0.0, slot, -1.0)
    row = iota((2 * MAIN, TOK), 0)
    wanted = jnp.where(row < MAIN, row, MAIN + lax.rem(row, REM)).astype(F32)
    for k in range(NZ):
        here = jnp.broadcast_to(slot[k : k + 1, :], (2 * MAIN, TOK)) == wanted
        place[k * 2 * MAIN : (k + 1) * 2 * MAIN, :] = jnp.where(here, 1.0, 0.0).astype(BF16)
    my_slot = jnp.sum(jnp.where(number == e, slot, 0.0), axis=0, keepdims=True)
    by_token = jnp.where(
        jnp.broadcast_to(my_slot, (HEAD, TOK)) == iota((HEAD, TOK), 0).astype(F32), 1.0, 0.0
    ).astype(BF16)
    eye = jnp.where(iota((TOK, TOK), 0) == iota((TOK, TOK), 1), 1.0, 0.0)
    slot_of_token = lax.dot_general(eye.astype(BF16), by_token, NT, preferred_element_type=F32)

    r256, l256 = iota((256, 256), 0), iota((256, 256), 1)
    i64 = lax.rem(r256, 64)
    to_unit = lax.div(i64, REM) * 16 + lax.div(r256, 64) * REM + lax.rem(i64, REM)
    perm[...] = jnp.where(l256 == to_unit, 1.0, 0.0).astype(BF16)
    to_flat = lax.rem(lax.div(r256, REM), 4) * 64 + lax.div(r256, 16) * REM + lax.rem(r256, REM)
    unperm[...] = jnp.where(l256 == to_flat, 1.0, 0.0).astype(BF16)

    gate_acc[...] = jnp.zeros_like(gate_acc)
    up_acc[...] = jnp.zeros_like(up_acc)
    half = COLS // 2
    stats[e] = jnp.zeros((2 * NZ, 128), F32)
    top[...] = jnp.full(top.shape, -1e30, F32)
    tot[...] = jnp.zeros_like(tot)
    acc[...] = jnp.zeros_like(acc)

    loads[0].wait()
    for g in range(GROUPS):
        qs[g * TOK : (g + 1) * TOK, :] = qv[:, g * HEAD : (g + 1) * HEAD]

    klane, vlane = slice(0, HEAD), slice(HEAD, 2 * HEAD)

    def row_wait(db, bb):
        for da in range(4):
            if da + db > 0:
                wait(kv.at[kv_rows(core, bb, lax.rem(a + 4 - da, 4)), :], kvr.at[db * 4 + da])

    def row_pass(i, bb):
        rows = kv.at[kv_rows(core, bb, 0, 4), :]
        remote(rows, rows, kvs.at[15 + i], kvr.at[16 + i], to_sib).start()

    query_pos = c * TOK + lax.rem(iota((GROUPS * TOK, 1), 0), TOK)
    lane = iota((1, BUNDLE), 1)
    score_scale = 1.0 / math.sqrt(HEAD)

    def attend(kk, bb):
        rows = kv_rows(kk, bb, 0, 4)
        key_pos = (
            TOK * kk
            + lax.rem(lane, TOK)
            + 2 * TOK * ((1 + 3 * kk) * lax.div(lane, TOK) + (4 - 3 * kk) * bb)
        )
        scores = (
            lax.dot_general(qs[...], kv[rows, klane], NT, preferred_element_type=F32) * score_scale
        )
        allowed = key_pos <= query_pos
        if SEQ > WINDOW:
            allowed = allowed & (key_pos > query_pos - WINDOW)
        scores = jnp.where(allowed, scores, -1e30)
        old = top[:, 0:1]
        new = jnp.maximum(old, jnp.max(scores, axis=1, keepdims=True))
        fade = jnp.exp(old - new)
        weights = jnp.exp(scores - new)
        top[...] = jnp.broadcast_to(new, top.shape)
        tot[...] = tot[...] * fade + jnp.sum(weights, axis=1, keepdims=True)
        acc[...] = acc[...] * fade + jnp.dot(
            weights.astype(BF16), kv[rows, vlane], preferred_element_type=F32
        )

    def other_wait(i, aa):
        wait(kv.at[kv_rows(1 - core, aa, 0, 4), :], kvr.at[16 + i])

    row_wait(0, b)
    row_pass(0, b)
    attend(core, b)
    other_wait(0, a)
    attend(1 - core, a)
    row_wait(1, bm)
    row_pass(1, bm)
    row_wait(3, bp)
    row_pass(2, bp)
    attend(core, bm)
    attend(core, bp)
    row_wait(2, b2)
    row_pass(3, b2)
    for i, (src, dst) in enumerate(((wg_ref, wg), (wu_ref, wu), (wd_ref, wd))):
        remote(src.at[0], dst.at[FF : 2 * FF], ws.at[i], wr.at[i], to_sib).start()
    other_wait(1, am)
    attend(1 - core, am)
    other_wait(2, ap)
    attend(1 - core, ap)
    attend(core, b2)
    other_wait(3, a2)
    attend(1 - core, a2)

    for g in range(GROUPS):
        rows = slice(g * TOK, (g + 1) * TOK)
        attn[:, g * HEAD : (g + 1) * HEAD] = (acc[rows, :] / tot[rows, 0:1]).astype(BF16)

    def cols(j):
        return pl.ds(pl.multiple_of(j * COLS, COLS), COLS)

    def project(s):
        return jnp.dot(attn[...], wo[:, cols(chunk(s))], preferred_element_type=F32)

    lo, hi = slice(0, half), slice(half, COLS)
    full = slice(0, COLS)
    moves = (
        (0, lo, 0, 2), (0, hi, 7, -2), (1, full, 1, 1), (2, full, 2, -1), (3, full, 3, 1), (4, full, 4, -1),
        (5, full, 5, 2), (6, full, 6, -2),
    )

    def sum_send(k):
        i, lanes, sem, step = moves[k]
        remote(
            zs.at[i, :, lanes], zr.at[i, :, lanes], z1s.at[sem], z1r.at[sem], to_z(step)
        ).start()

    def sum_wait(k):
        i, lanes, sem, _ = moves[k]
        wait(zr.at[i, :, lanes], z1r.at[sem])

    loads[1].wait()
    zs[0] = project(4).astype(BF16)
    sum_send(0)
    sum_send(1)
    for i, s in ((1, 3), (2, -3), (3, 1), (4, -1)):
        zs[i] = project(s).astype(BF16)
        sum_send(i + 1)
    up, down = project(2), project(-2)
    loads[2].wait()
    total = project(0) + res[...].astype(F32)
    sum_wait(2)
    sum_wait(0)
    up = up + zr[1].astype(F32)
    zs[5, :, lo] = (up[:, lo] + zr[0, :, lo].astype(F32)).astype(BF16)
    zs[5, :, hi] = up[:, hi].astype(BF16)
    sum_send(6)
    sum_wait(3)
    sum_wait(1)
    down = down + zr[2].astype(F32)
    zs[6, :, hi] = (down[:, hi] + zr[0, :, hi].astype(F32)).astype(BF16)
    zs[6, :, lo] = down[:, lo].astype(BF16)
    sum_send(7)
    sum_wait(4)
    sum_wait(5)
    total = total + zr[3].astype(F32) + zr[4].astype(F32)
    sum_wait(6)
    sum_wait(7)
    total = (total + zr[5].astype(F32) + zr[6].astype(F32)).astype(BF16)
    att[e] = total

    loads[6].wait()
    loads[7].wait()
    def unit(aa, bb):
        return pl.ds(pl.multiple_of((bb * 4 + aa) * MAIN, MAIN), MAIN)

    tile = lax.div(iota((MAIN, 128), 0), REM)
    value = total.astype(F32)
    scaled = (value * gain_ref[:, cols(e)]).astype(BF16)
    packed = jnp.dot(place[...], scaled, preferred_element_type=F32)
    for k in range(NZ):
        at = k * 2 * MAIN
        zunits[k, :, 0:COLS] = packed[at : at + MAIN].astype(BF16)
        rest = jnp.zeros((MAIN, 128), F32)
        for t in range(4):
            rest = rest + jnp.where(
                tile == t, packed[at + MAIN : at + 2 * MAIN, t * 128 : (t + 1) * 128], 0.0
            )
        zunits[k, :, COLS:UNIT] = rest.astype(BF16)
    spread_steps = ((1, 2), (-1, 1), (2, 4), (-2, 3), (3, 6), (-3, 5), (4, 7))
    first_steps = ((1, 0), (3, 1), (2, 2))
    mine_rows = unit(a, b)
    for s, n in spread_steps:
        src, dst = zunits.at[chunk(s)], slots.at[e, mine_rows, :]
        remote(src, dst, zas.at[n], zar.at[n], to_z(s)).start()
        if n < 3:
            for da, i in first_steps:
                device = (ctx_of(*at_step(da, 0)), chunk(s))
                remote(src, dst, ags.at[i, n], agr.at[i, n], device).start()
    slots[e, mine_rows, :] = zunits[e]
    here = slots.at[e, mine_rows, :]
    for da, i in first_steps:
        remote(here, here, ags.at[i, 0], agr.at[i, 0], (ctx_of(*at_step(da, 0)), e)).start()
    squares = jnp.sum(value * value, axis=1, keepdims=True)
    stats[e, 0:NZ, 0:TOK] = lax.dot_general(
        rt_ref[:, cols(e)], scaled, NT, preferred_element_type=F32
    )
    stats[e, NZ : 2 * NZ, 0:TOK] = jnp.broadcast_to(
        jnp.sum(eye * squares, axis=0, keepdims=True), (NZ, TOK)
    )

    def ag_chunk(n):
        odd = lax.rem(n, 2)
        return chunk((2 * odd - 1) * lax.div(n + 1, 2))

    def bundle(bb):
        return pl.ds(pl.multiple_of(bb * 64, 64), 64)

    def first_half(bb):
        return pl.ds(pl.multiple_of(bb * 64, 32), 32)

    def second_half(bb):
        return pl.ds(pl.multiple_of(bb * 64 + 32, 32), 32)

    def scale_unit(aa, bb):
        return pl.ds(pl.multiple_of((bb * 4 + aa) * 8, 8), 8)

    def scale_bundle(bb):
        return pl.ds(pl.multiple_of(bb * 32, 8), 32)

    def out_copy(j):
        return pltpu.make_async_copy(att.at[j], att_out.at[:, cols(j)], outs.at[j])

    def token_stats():
        whole = stats[0]
        for k in range(1, NZ):
            whole = whole + stats[k]
        inverse = lax.rsqrt(whole[NZ : NZ + 1, 0:TOK] * (1.0 / D) + 1e-05)
        return whole[0:NZ, 0:TOK] * inverse, inverse

    def stats_send():
        for s, k in spread_steps:
            remote(stats.at[e], stats.at[e], sts.at[k], str_.at[k], to_z(s)).start()

    def columns_send():
        for s, k in spread_steps:
            remote(att.at[e], att.at[e], ats.at[k], atr.at[k], to_z(s)).start()

    def ag_start(n):
        here = slots.at[ag_chunk(n), mine_rows, :]
        wait(here, zar.at[n])
        remote(here, here, ags.at[0, n], agr.at[0, n], to_ap).start()
        remote(here, here, ags.at[1, n], agr.at[1, n], to_am).start()
        remote(here, here, ags.at[2, n], agr.at[2, n], to_a2).start()

    def scale_start():
        for k in range(1, NZ):
            wait(stats.at[ag_chunk(k)], str_.at[k])
        inverse = token_stats()[1]
        inverse = jnp.sum(eye * inverse, axis=1, keepdims=True)
        by_slot = jnp.sum(slot_of_token * inverse, axis=0, keepdims=True)
        scales[scale_unit(a, b), :] = jnp.broadcast_to(by_slot, (8, HEAD))
        here = scales.at[scale_unit(a, b), :]
        remote(here, here, scs.at[0], scr.at[0], to_ap).start()
        remote(here, here, scs.at[1], scr.at[1], to_am).start()
        remote(here, here, scs.at[2], scr.at[2], to_a2).start()

    def scale_second():
        wait(scales.at[scale_unit(am, b), :], scr.at[0])
        wait(scales.at[scale_unit(ap, b), :], scr.at[1])
        wait(scales.at[scale_unit(a2, b), :], scr.at[2])
        piece = scales.at[scale_bundle(b), :]
        remote(piece, piece, scs.at[3], scr.at[3], to_bp).start()
        remote(piece, piece, scs.at[4], scr.at[4], to_bm).start()
        remote(piece, piece, scs.at[5], scr.at[5], to_b2).start()

    def ag_second(n):
        j = ag_chunk(n)
        if isinstance(n, int) and 0 < n < 3:
            wait(slots.at[j, mine_rows, :], zar.at[n])
        wait(slots.at[j, unit(am, b), :], agr.at[0, n])
        wait(slots.at[j, unit(ap, b), :], agr.at[1, n])
        wait(slots.at[j, unit(a2, b), :], agr.at[2, n])
        piece = slots.at[j, bundle(b), :]
        remote(piece, piece, ags.at[3, n], agr.at[3, n], to_bp).start()
        remote(piece, piece, ags.at[4, n], agr.at[4, n], to_bm).start()

        @pl.when(n >= AG_RELAYED)
        def _():
            remote(piece, piece, ags.at[5, n], agr.at[5, n], to_b2).start()

    def ag_third(n):
        j = ag_chunk(n)

        wait(slots.at[j, bundle(bm), :], agr.at[3, n])
        piece = slots.at[j, first_half(bm), :]
        remote(piece, piece, ags.at[5, n], agr.at[5, n], to_bp).start()
        wait(slots.at[j, bundle(bp), :], agr.at[4, n])
        piece = slots.at[j, second_half(bp), :]
        remote(piece, piece, ags.at[6, n], agr.at[6, n], to_bm).start()

    def ag_use(n):
        j = ag_chunk(n)

        @pl.when(n < AG_RELAYED)
        def _():
            wait(slots.at[j, first_half(b2), :], agr.at[5, n])
            wait(slots.at[j, second_half(b2), :], agr.at[6, n])

        @pl.when(n >= AG_RELAYED)
        def _():
            wait(slots.at[j, bundle(bm), :], agr.at[3, n])
            wait(slots.at[j, bundle(bp), :], agr.at[4, n])
            wait(slots.at[j, bundle(b2), :], agr.at[5, n])

        flat = jnp.dot(
            perm[...], slots[j, 0:256, COLS:UNIT], preferred_element_type=F32
        ).astype(BF16)
        for t in range(4):
            slots[j, 256:ROWS, t * 128 : (t + 1) * 128] = flat[t * 64 : (t + 1) * 64]
        rows = slots[j, :, 0:COLS]
        gate_acc[...] += lax.dot_general(rows, wg[:, cols(j)], NT, preferred_element_type=F32)
        up_acc[...] += lax.dot_general(rows, wu[:, cols(j)], NT, preferred_element_type=F32)

    def run(stages, count):
        last = max(lag for _, lag in stages)

        def tick(t, carry):
            for function, lag in stages:

                @pl.when((t >= lag) & (t < lag + count))
                def _(function=function, lag=lag):
                    function(t - lag)

            return carry

        lax.fori_loop(0, count + last, tick, 0)

    stats_send()
    ag_second(0)
    ag_second(1)
    ag_start(3)
    ag_start(4)
    ag_second(2)
    ag_start(5)
    ag_start(6)
    ag_start(7)
    ag_third(0)
    ag_second(3)
    ag_third(1)
    ag_second(4)
    ag_second(5)
    ag_third(2)
    ag_second(6)
    ag_third(3)
    ag_second(7)
    ag_third(4)
    scale_start()
    columns_send()

    loads[3].wait()
    loads[4].wait()
    wait(wg.at[FF : 2 * FF], wr.at[0])
    wait(wu.at[FF : 2 * FF], wr.at[1])
    def ag_tick(n, carry):
        @pl.when(n + 5 < AG_RELAYED)
        def _():
            ag_third(n + 5)

        ag_use(n)

        @pl.when(n == 2)
        def _():
            scale_second()

        return carry

    lax.fori_loop(0, NZ, ag_tick, 0)
    wait(scales.at[scale_bundle(bm), :], scr.at[3])
    wait(scales.at[scale_bundle(bp), :], scr.at[4])
    wait(scales.at[scale_bundle(b2), :], scr.at[5])

    row = iota((ROWS, HEAD), 0)
    col = iota((ROWS, HEAD), 1)
    over = row - 256
    block_of = jnp.where(row < 256, lax.div(row, MAIN), lax.div(over, REM))
    slot_of = jnp.where(row < 256, lax.rem(row, MAIN), MAIN + lax.rem(over + 256, REM))
    pick = jnp.where(col == block_of * 8, 1.0, 0.0)
    spread = jnp.dot(pick, scales[...], precision=HIGH, preferred_element_type=F32)
    factor = jnp.sum(jnp.where(col == slot_of, spread, 0.0), axis=1, keepdims=True)
    gated = gate_acc[...] * factor
    hid[...] = (gated / (1.0 + jnp.exp(-gated)) * (up_acc[...] * factor)).astype(BF16)
    loads[5].wait()
    wait(wd.at[FF : 2 * FF], wr.at[2])

    def rs_chunk(n):
        odd = lax.rem(n, 2)
        return chunk(odd * (4 - lax.div(n + 1, 2)) - (1 - odd) * (4 - lax.div(n, 2)))

    def rs_start(n):
        j = rs_chunk(n)
        out = jnp.dot(hid[...], wd[:, cols(j)], preferred_element_type=F32).astype(BF16)
        part[n, :, 0:COLS] = out[0:256]
        rest = jnp.concatenate([out[256:, t * 128 : (t + 1) * 128] for t in range(4)], axis=0)
        part[n, :, COLS:UNIT] = jnp.dot(unperm[...], rest, preferred_element_type=F32).astype(BF16)

        @pl.when(n < RS_RELAYED)
        def _():
            remote(
                part.at[n, first_half(b2), :], r1p.at[n], rss.at[0, n], rsr.at[0, n], to_bp
            ).start()
            remote(
                part.at[n, second_half(b2), :], r1m.at[n], rss.at[1, n], rsr.at[1, n], to_bm
            ).start()

        @pl.when(n >= RS_RELAYED)
        def _():
            remote(part.at[n, bundle(b2), :], r2x.at[n], rss.at[0, n], rsr.at[0, n], to_b2).start()
            remote(part.at[n, bundle(bp), :], r2p.at[n], rss.at[2, n], rsr.at[2, n], to_bp).start()
            remote(part.at[n, bundle(bm), :], r2m.at[n], rss.at[3, n], rsr.at[3, n], to_bm).start()

        @pl.when(n == 7)
        def _():
            logits = token_stats()[0]
            one = jnp.sum(jnp.where(number == first_id, logits, 0.0), axis=0, keepdims=True)
            two = jnp.sum(jnp.where(number == second_id, logits, 0.0), axis=0, keepdims=True)
            gate = 1.0 / (1.0 + jnp.exp(two - one))
            gates = jnp.where(first_id == number, gate, 1.0 - gate)
            spread = jnp.concatenate(
                [jnp.broadcast_to(gates[k : k + 1, :], (2 * MAIN, TOK)) for k in range(NZ)], axis=0
            )
            spread = spread * place[...].astype(F32)
            turned = lax.dot_general(eye, spread, NT, precision=HIGH, preferred_element_type=F32)
            high = turned.astype(BF16)
            wgt_hi[...] = high
            wgt_lo[...] = (turned - high.astype(F32)).astype(BF16)

    def add(n, rows, lanes, more):
        value = part[n, rows, lanes].astype(F32)
        for term in more:
            value = value + term.astype(F32)
        return value

    every = slice(0, UNIT)

    def rs_first(n):
        @pl.when(n < RS_RELAYED)
        def _():
            wait(r1p.at[n], rsr.at[0, n])
            rows = first_half(bp)
            part[n, rows, every] = add(n, rows, every, [r1p[n]]).astype(BF16)
            remote(part.at[n, bundle(bp), :], r2p.at[n], rss.at[2, n], rsr.at[2, n], to_bp).start()
            wait(r1m.at[n], rsr.at[1, n])
            rows = second_half(bm)
            part[n, rows, every] = add(n, rows, every, [r1m[n]]).astype(BF16)
            remote(part.at[n, bundle(bm), :], r2m.at[n], rss.at[3, n], rsr.at[3, n], to_bm).start()

    def rs_second(n):
        @pl.when(n > 0)
        def _():
            wait(att.at[ag_chunk(n)], atr.at[n])

        out_copy(ag_chunk(n)).start()
        wait(r2p.at[n], rsr.at[2, n])
        wait(r2m.at[n], rsr.at[3, n])
        rows = bundle(b)

        @pl.when(n < RS_RELAYED)
        def _():
            part[n, rows, every] = add(n, rows, every, [r2p[n], r2m[n]]).astype(BF16)

        @pl.when(n >= RS_RELAYED)
        def _():
            wait(r2x.at[n], rsr.at[0, n])
            part[n, rows, every] = add(n, rows, every, [r2p[n], r2m[n], r2x[n]]).astype(BF16)

        remote(part.at[n, unit(ap, b), :], r4p.at[n], rss.at[5, n], rsr.at[5, n], to_ap).start()
        remote(part.at[n, unit(am, b), :], r4m.at[n], rss.at[6, n], rsr.at[6, n], to_am).start()
        remote(part.at[n, unit(a2, b), :], r4x.at[n], rss.at[4, n], rsr.at[4, n], to_a2).start()

    def rs_last(n):
        wait(r4p.at[n], rsr.at[5, n])
        wait(r4m.at[n], rsr.at[6, n])
        wait(r4x.at[n], rsr.at[4, n])
        zout[n] = add(n, unit(a, b), every, [r4p[n], r4m[n], r4x[n]]).astype(BF16)

        @pl.when(n < 7)
        def _():
            remote(zout.at[n], fin.at[e], z2s.at[n], z2r.at[7 - n], (c, rs_chunk(n))).start()

        @pl.when(n == 7)
        def _():
            fin[e] = zout[7]

    run(((rs_start, 0),), NZ)
    run(((rs_last, 12), (rs_second, 7), (rs_first, 0)), NZ)

    for n in range(1, NZ):
        wait(fin.at[ag_chunk(n)], z2r.at[n])
    for k in range(NZ):
        at = k * 2 * MAIN
        terms[at : at + MAIN, :] = fin[k, :, 0:COLS]
        rest = fin[k, :, COLS:UNIT].astype(F32)
        for t in range(4):
            terms[at + MAIN : at + 2 * MAIN, t * 128 : (t + 1) * 128] = jnp.where(
                tile == t, rest, 0.0
            ).astype(BF16)
    mixed = jnp.dot(wgt_hi[...], terms[...], preferred_element_type=F32)
    mixed = mixed + jnp.dot(wgt_lo[...], terms[...], preferred_element_type=F32)
    mixed_out[...] = mixed.astype(BF16)
    mix_copy = pltpu.make_async_copy(mixed_out, mix_out, ld.at[11])
    mix_copy.start()

    for i in range(15):
        wait(mine_kv, kvs.at[i])
    for i in range(4):
        wait(kv.at[0 : 4 * TOK, :], kvs.at[15 + i])
    for i, ref in enumerate((wg, wu, wd)):
        wait(ref.at[FF : 2 * FF], ws.at[i])
    for i, lanes, sem, _ in moves:
        wait(zs.at[i, :, lanes], z1s.at[sem])


    def drain(n, carry):
        for i, rows in enumerate((MAIN, MAIN, MAIN, 64, 64)):
            wait(slots.at[0, 0:rows, :], ags.at[i, n])

        @pl.when(n < AG_RELAYED)
        def _():
            wait(slots.at[0, 0:32, :], ags.at[5, n])
            wait(slots.at[0, 0:32, :], ags.at[6, n])

        @pl.when(n >= AG_RELAYED)
        def _():
            wait(slots.at[0, 0:64, :], ags.at[5, n])

        @pl.when(n < RS_RELAYED)
        def _():
            wait(r1p.at[0], rss.at[0, n])
            wait(r1p.at[0], rss.at[1, n])

        @pl.when(n >= RS_RELAYED)
        def _():
            wait(r2x.at[0], rss.at[0, n])

        for i, piece in ((2, r2p), (3, r2m), (4, r4x), (5, r4p), (6, r4m)):
            wait(piece.at[0], rss.at[i, n])

        @pl.when(n < 7)
        def _():
            wait(zout.at[0], z2s.at[n])
            wait(zunits.at[0], zas.at[n + 1])
            wait(stats.at[0], sts.at[n + 1])
            wait(att.at[0], ats.at[n + 1])

        out_copy(n).wait()
        return carry

    lax.fori_loop(0, NZ, drain, 0)
    for i in range(6):
        wait(scales.at[0:8, :] if i < 3 else scales.at[0:32, :], scs.at[i])
    mix_copy.wait()


def hand_on(att_in, mix_in, att_out, mix_out, att_near, mix_near, sem):
    parts = [(mix_in, mix_near, mix_out, slice(0, TOK))]
    parts += [(att_in, att_near, att_out, slice(at, at + 32)) for at in range(0, TOK, 32)]
    ins = [
        pltpu.make_async_copy(src.at[rows, :], near.at[rows, :], sem.at[0, i])
        for i, (src, near, _, rows) in enumerate(parts)
    ]
    outs = [
        pltpu.make_async_copy(near.at[rows, :], dst.at[rows, :], sem.at[1, i])
        for i, (_, near, dst, rows) in enumerate(parts)
    ]
    for copy in ins:
        copy.start()
    for copy, out in zip(ins, outs):
        copy.wait()
        out.start()
    for out in outs:
        out.wait()


def local(
    query, key_states, value_states, residual, out_weight, norm_gain, router_weight, expert_ids,
    gate_weight, up_weight, down_weight,
):
    anywhere = pl.BlockSpec(memory_space=pl.ANY)
    vmem = pltpu.VMEM
    dma = pltpu.SemaphoreType.DMA
    scratch = [
        vmem((1, D), F32),
        vmem((NZ, D), BF16),
        vmem((2, TOK), jnp.int32),
        vmem((TOK, COLS), BF16),
        vmem((TOK, GROUPS * HEAD), BF16),
        vmem((SEQ, 2 * HEAD), BF16),
        vmem((GROUPS * TOK, HEAD), BF16),
        vmem((GROUPS * TOK, HEAD), F32),
        vmem((GROUPS * TOK, HEAD), F32),
        vmem((GROUPS * TOK, HEAD), F32),
        vmem((TOK, GROUPS * HEAD), BF16),
        vmem((GROUPS * HEAD, D), BF16),
        vmem((TOK, COLS), BF16),
        vmem((2 * FF, D), BF16),
        vmem((2 * FF, D), BF16),
        vmem((2 * FF, D), BF16),
        vmem((7, TOK, COLS), BF16),
        vmem((7, TOK, COLS), BF16),
        vmem((NZ, TOK, COLS), BF16),
        vmem((NZ, 2 * NZ, 128), F32),
        vmem((NZ * 2 * MAIN, TOK), BF16),
        vmem((256, 256), BF16),
        vmem((256, 256), BF16),
        vmem((NZ, MAIN, UNIT), BF16),
        vmem((NZ, ROWS, UNIT), BF16),
        vmem((NB * 8, HEAD), F32),
        vmem((ROWS, 2 * FF), F32),
        vmem((ROWS, 2 * FF), F32),
        vmem((ROWS, 2 * FF), BF16),
        vmem((TOK, NZ * 2 * MAIN), BF16),
        vmem((TOK, NZ * 2 * MAIN), BF16),
        vmem((NZ, 256, UNIT), BF16),
        vmem((NZ, 32, UNIT), BF16),
        vmem((NZ, 32, UNIT), BF16),
        vmem((NZ, 64, UNIT), BF16),
        vmem((NZ, 64, UNIT), BF16),
        vmem((NZ, 64, UNIT), BF16),
        vmem((NZ, MAIN, UNIT), BF16),
        vmem((NZ, MAIN, UNIT), BF16),
        vmem((NZ, MAIN, UNIT), BF16),
        vmem((NZ, MAIN, UNIT), BF16),
        vmem((NZ, MAIN, UNIT), BF16),
        vmem((NZ * 2 * MAIN, COLS), BF16),
        dma((12,)),
        dma((19,)),
        dma((20,)),
        dma((3,)),
        dma((3,)),
        dma((8,)),
        dma((8,)),
        dma((8,)),
        dma((8,)),
        dma((15,)),
        dma((16,)),
        dma((8,)),
        dma((8,)),
        dma((8,)),
        dma((8,)),
        dma((7, NZ)),
        dma((7, NZ)),
        dma((6,)),
        dma((6,)),
        dma((7, NZ)),
        dma((7, NZ)),
        dma((8,)),
        dma((8,)),
        dma((NZ,)),
    ]
    results = pl.pallas_call(
        kernel,
        out_shape=(
            jax.ShapeDtypeStruct((TOK, D), BF16),
            jax.ShapeDtypeStruct((TOK, COLS), BF16),
        ),
        in_specs=[anywhere] * 11,
        out_specs=(anywhere, anywhere),
        scratch_shapes=scratch,
        compiler_params=pltpu.CompilerParams(
            collective_id=0, has_side_effects=True, vmem_limit_bytes=56 * 1024 * 1024
        ),
        name="layer",
    )(
        query,
        key_states,
        value_states,
        residual,
        out_weight,
        norm_gain.reshape(1, D),
        router_weight.T,
        expert_ids.T,
        jnp.swapaxes(gate_weight, 1, 2),
        jnp.swapaxes(up_weight, 1, 2),
        down_weight,
    )
    return pl.pallas_call(
        hand_on,
        out_shape=tuple(jax.ShapeDtypeStruct(r.shape, r.dtype) for r in results),
        in_specs=[anywhere] * 2,
        out_specs=(anywhere, anywhere),
        scratch_shapes=[vmem((TOK, D), BF16), vmem((TOK, COLS), BF16), dma((2, 5))],
        compiler_params=pltpu.CompilerParams(vmem_limit_bytes=60 * 1024 * 1024),
        name="hand_on",
    )(*results)


def solution(mesh):
    placed = (
        P("ctx", "exp"),
        P("ctx", "exp"),
        P("ctx", "exp"),
        P("ctx", None),
        P("exp", None),
        P(),
        P(),
        P("ctx", None),
        P("exp", None, "ctx"),
        P("exp", None, "ctx"),
        P("exp", "ctx", None),
    )
    return jax.shard_map(
        local,
        mesh=mesh,
        in_specs=placed,
        out_specs=(P("ctx", None), P("ctx", "exp")),
        check_vma=False,
    )
```
